32 devices in a mesh: side: 2 (over core), grp: 4 (over y, x), blk: 4 (over z).
Axes of the slice: x: 2, y: 2, z: 4, core: 2. Of those that a mesh axis runs over, the one named last changes fastest.
Arguments:
- node_modes: bfloat16 [3, 16384, 256], P(None, ('grp', 'blk'), 'side'), may hold values from -6 to 6
- node_index: int32 [4, 24576], P(None, ('grp', 'blk')), may hold values from 0 to 1023
- interp: float32 [4, 24576], P(None, ('grp', 'blk')), may hold values from 0.1 to 1
- normals: float32 [3, 24576], P(None, ('grp', 'blk')), may hold values from -6 to 6
- counts: int32 [16, 16], P(None, ('grp', 'blk')), may hold values from 0 to 96, as said below
- inverse_diag: bfloat16 [16384, 1024], P(('grp', 'blk'))
- lower_left: bfloat16 [16384, 32], P(('grp', 'blk')), may hold values from -0.375 to 0.375
- lower_right: bfloat16 [16384, 32], P(('grp', 'blk')), may hold values from -0.09375 to 0.09375
- upper_left: bfloat16 [16384, 32], P(('grp', 'blk')), may hold values from -0.375 to 0.375
- upper_right: bfloat16 [16384, 32], P(('grp', 'blk')), may hold values from -0.09375 to 0.09375
- ranks: int32 [16], P(('grp', 'blk')), may hold values from 8 to 32
- areas: float32 [16384], P(('grp', 'blk')), may hold values from 0.00390625 to 0.03125
Outputs:
- potentials: bfloat16 [16384, 256], P(('grp', 'blk'), 'side')
- added_mass: float32 [256, 256], P(('grp', 'blk'), 'side')
The draws below stay inside these ranges and needn't reach their ends.
Inputs may be any that keep to these rules, and one draw needn't show every extreme that they name: In each column d the counts sum to 1024, and every column holds one count equal to 96.
All inputs are finite; a program needn't handle non-finite values.
Results may differ from the reference program's by a relative error of at most 0.0049.
Values may be sent and summed in bfloat16 or wider, within the bound.
A program may use at most 64 MiB of HBM per device.

```python
import math
import jax
import jax.numpy as jnp
from jax import lax

MODES = 256
R = 32
PB = 1024
NODES_DEV = 1024
PANEL_DEVS = 16
PANELS = 16384
CAP = 96
SLOTS = 24576
SHELL_NODES = 16384


def draw_inverse_diag(key, part):
    key_one, key_two = jax.random.split(jax.random.fold_in(key, 101))
    diagonal = jax.random.uniform(key_one, (PANELS, 1), jnp.float32, 0.6, 1.4)
    off_terms = jax.random.normal(key_two, (PANELS, PB), jnp.float32) * (0.4 / jnp.sqrt(PB * 1.0))
    row_ids = lax.broadcasted_iota(jnp.int32, (PANELS, PB), 0) % PB
    col_ids = lax.broadcasted_iota(jnp.int32, (PANELS, PB), 1)
    return jnp.where(row_ids == col_ids, diagonal, off_terms).astype(jnp.bfloat16)


def draw_counts(key, part):

    def draw_column(column_id):
        column_key = jax.random.fold_in(jax.random.fold_in(key, 202), column_id)
        key_one, key_two = jax.random.split(column_key)
        forced_row = jax.random.randint(key_one, (), 0, PANEL_DEVS)
        ranking = jax.random.permutation(key_two, (PANEL_DEVS - 1) * CAP)
        picked = (ranking < PB - CAP).astype(jnp.int32).reshape(PANEL_DEVS - 1, CAP).sum(axis=1)
        sources = jnp.arange(PANEL_DEVS, dtype=jnp.int32)
        moved = jnp.clip(jnp.where(sources > forced_row, sources - 1, sources), 0, PANEL_DEVS - 2)
        return jnp.where(sources == forced_row, CAP, picked[moved]).astype(jnp.int32)
    columns = jax.vmap(draw_column)(jnp.arange(PANEL_DEVS, dtype=jnp.int32))
    return columns.T.astype(jnp.int32)


def with_ends(entries, stream_key, least, high):
    spot = [jax.random.randint(jax.random.fold_in(stream_key, axis), (), 0, length) for axis, length in enumerate(entries.shape)]
    widest = entries.shape.index(max(entries.shape))
    next_to = spot[:widest] + [(spot[widest] + 1) % entries.shape[widest]] + spot[widest + 1:]
    return entries.at[tuple(spot)].set(least).at[tuple(next_to)].set(high)


def block_levels(key, extent, shards, smallest, top_value):
    loudness, own = 1.0, jax.random.fold_in(key, 6)
    for dim, blocks in shards:
        draws = jnp.exp(jax.random.uniform(jax.random.fold_in(own, dim), (blocks,), jnp.float32, smallest / len(shards), top_value / len(shards)))
        loudness = loudness * jnp.repeat(draws, extent[dim] // blocks).reshape([-1 if axis == dim else 1 for axis in range(len(extent))])
    return loudness


def normal_values(stream_key, dims, scale, limit, pieces=(), held_as=jnp.bfloat16):
    entries = jax.random.normal(stream_key, dims, jnp.float32) * scale
    if len(pieces) > 0:
        entries = block_levels(stream_key, dims, pieces, -0.22, 0.18) * entries
    return jnp.clip(entries, min=-limit, max=limit).astype(held_as)


def setup_inputs(seed: int = 0) -> dict:
    splits = jax.random.split(jax.random.key(seed), 13)
    return {
        "node_modes": normal_values(splits[0], (3, SHELL_NODES, MODES), 1.0, 6.0, ((1, 16), (2, 2))),
        "node_index": with_ends(jax.random.randint(splits[1], (4, SLOTS), 0, NODES_DEV), jax.random.fold_in(splits[1], 1), 0, NODES_DEV - 1).astype(jnp.int32),
        "interp": jnp.clip(0.1 + 0.9 * jax.random.uniform(splits[2], (4, SLOTS), jnp.float32) ** block_levels(splits[2], (4, SLOTS), ((1, 16),), -0.2, 0.2), 0.1, 1.0),
        "normals": normal_values(splits[3], (3, SLOTS), 1.0, 6.0, ((1, 16),), jnp.float32),
        "counts": draw_counts(jax.random.fold_in(splits[12], 71), 0),
        "inverse_diag": draw_inverse_diag(jax.random.fold_in(splits[12], 71), 0),
        "lower_left": normal_values(splits[6], (PANELS, R), (PB // 4) ** -0.5, 0.375, ((0, 16),)),
        "lower_right": normal_values(splits[7], (PANELS, R), (PB * PANEL_DEVS // 4) ** -0.5, 0.09375, ((0, 16),)),
        "upper_left": normal_values(splits[8], (PANELS, R), (PB // 4) ** -0.5, 0.375, ((0, 16),)),
        "upper_right": normal_values(splits[9], (PANELS, R), (PB * PANEL_DEVS // 4) ** -0.5, 0.09375, ((0, 16),)),
        "ranks": with_ends(jax.random.randint(splits[10], (PANEL_DEVS,), R // 4, R + 1), jax.random.fold_in(splits[10], 1), R // 4, R).astype(jnp.int32),
        "areas": jnp.clip(jnp.exp(math.log(0.03125) - 2.0794415 * jax.random.uniform(splits[11], (PANELS,), jnp.float32) ** block_levels(splits[11], (PANELS,), ((0, 16),), -0.2, 0.2)), 0.00390625, 0.03125),
    }


HIGH = lax.Precision.HIGHEST


def shell_rows(node_modes, node_index, interp, normals, source_id):
    span = PANEL_DEVS * CAP
    local_modes = lax.dynamic_slice_in_dim(node_modes, source_id * NODES_DEV, NODES_DEV, 1)
    start_slot = source_id * span
    local_index = lax.dynamic_slice_in_dim(node_index, start_slot, span, 1)
    local_interp = lax.dynamic_slice_in_dim(interp, start_slot, span, 1)
    local_normals = lax.dynamic_slice_in_dim(normals, start_slot, span, 1)
    velocity = jnp.zeros((span, MODES), jnp.float32)
    for corner in range(4):
        picked = jnp.take(local_modes, local_index[corner], axis=1)
        for axis_id in range(3):
            weight_now = local_interp[corner] * local_normals[axis_id]
            velocity = velocity + weight_now[:, None] * picked[axis_id].astype(jnp.float32)
    return velocity.astype(jnp.bfloat16)


def reference(node_modes, node_index, interp, normals, counts, inverse_diag, lower_left, lower_right, upper_left, upper_right, ranks, areas):
    source_ids = jnp.arange(PANEL_DEVS, dtype=jnp.int32)
    velocity = lax.map(lambda source_id: shell_rows(node_modes, node_index, interp, normals, source_id), source_ids)
    velocity = velocity.reshape(PANEL_DEVS, PANEL_DEVS, CAP, MODES)

    def place(block_id):
        column = counts[:, block_id]
        cum_ends = jnp.cumsum(column).astype(jnp.int32)
        cum_starts = cum_ends - column
        position = jnp.arange(PB, dtype=jnp.int32)
        owner = jnp.sum((cum_ends[None, :] <= position[:, None]).astype(jnp.int32), axis=1)
        slot_pos = position - cum_starts[owner]
        return velocity[owner, block_id, slot_pos]

    normal_velocity = lax.map(place, source_ids)
    mask_cols = jnp.arange(R, dtype=jnp.int32)

    def forward(carried, inputs):
        inverse_block, left_block, right_block, rank_now, rhs_block = inputs
        keep = (mask_cols < rank_now)[None, :]
        left_masked = jnp.where(keep, left_block, jnp.zeros_like(left_block))
        solved = jnp.dot(inverse_block, rhs_block, preferred_element_type=jnp.float32)
        spread = jnp.dot(inverse_block, left_masked, preferred_element_type=jnp.float32)
        interim = solved - jnp.dot(spread, carried, precision=HIGH)
        carried = carried + jnp.dot(right_block.astype(jnp.float32).T, interim, precision=HIGH)
        return carried, interim

    inputs = (inverse_diag.reshape(PANEL_DEVS, PB, PB), lower_left.reshape(PANEL_DEVS, PB, R), lower_right.reshape(PANEL_DEVS, PB, R), ranks, normal_velocity)
    ignored, interim = lax.scan(forward, jnp.zeros((R, MODES), jnp.float32), inputs)

    def backward(carried, inputs):
        left_block, right_block, rank_now, interim_block = inputs
        keep = (mask_cols < rank_now)[None, :]
        left_masked = jnp.where(keep, left_block, jnp.zeros_like(left_block)).astype(jnp.float32)
        result = interim_block - jnp.dot(left_masked, carried, precision=HIGH)
        carried = carried + jnp.dot(right_block.astype(jnp.float32).T, result, precision=HIGH)
        return carried, result

    inputs = (upper_left.reshape(PANEL_DEVS, PB, R), upper_right.reshape(PANEL_DEVS, PB, R), ranks, interim)
    ignored, result = lax.scan(backward, jnp.zeros((R, MODES), jnp.float32), inputs, reverse=True)
    potentials = result.reshape(PANELS, MODES).astype(jnp.bfloat16)
    weighted = (areas[:, None] * potentials.astype(jnp.float32)).astype(jnp.bfloat16)
    flat_velocity = normal_velocity.reshape(PANELS, MODES)
    added_mass = jnp.dot(flat_velocity.T, weighted, preferred_element_type=jnp.float32)
    return potentials, added_mass
```

```python
import functools

import jax
import jax.numpy as jnp
from jax import lax
from jax.experimental import pallas as pl
from jax.experimental.pallas import tpu as pltpu
from jax.sharding import PartitionSpec as P

MESH = pl.DeviceIdType.MESH
F32 = jnp.float32
BF16 = jnp.bfloat16
TILE = 16


def dot(a, b):
    return jnp.dot(a, b, preferred_element_type=F32)


def dot_rows(a, b):
    return lax.dot_general(a, b, (((0,), (0,)), ((), ())), preferred_element_type=F32)


def split(a):
    high = a.astype(BF16)
    return high, (a - high.astype(F32)).astype(BF16)


def kernel(
    ng,
    nb,
    cap,
    out_rows,
    modes_hbm,
    index_hbm,
    interp_hbm,
    normals_hbm,
    counts,
    diag_hbm,
    ll_hbm,
    lr_hbm,
    ul_hbm,
    ur_hbm,
    ranks,
    areas_hbm,
    pot_hbm,
    mass_ref,
    modes,
    index,
    interp,
    normals,
    diag,
    ll,
    lr,
    ul,
    ur,
    areas,
    rows_pack,
    cols,
    wbuf,
    sendbuf,
    arrived,
    pick,
    maps,
    back_terms,
    kout,
    wcat,
    gp,
    solved,
    velocities,
    velocities_t,
    zall,
    psend,
    precv,
    pot,
    msend,
    mrecv,
    local_sem,
    map_send,
    map_recv,
    slab_send,
    slab_recv,
    vel_send,
    vel_recv,
    side_send,
    side_recv,
    z_send,
    z_recv,
    p_send,
    p_recv,
    m_send,
    m_recv,
):
    nd = ng * nb
    rank_width = ll.shape[1]
    two = 2 * rank_width
    panels = diag.shape[0]
    nodes, width3 = modes.shape
    width = width3 // 3
    slots = nd * cap
    side, my_g, my_b = lax.axis_index("side"), lax.axis_index("grp"), lax.axis_index("blk")
    me = my_g * nb + my_b

    barrier = pltpu.get_barrier_semaphore()

    @pl.loop(1, nd)
    def _(k):
        other = lax.rem(me + k, nd)
        pl.semaphore_signal(
            barrier, inc=1, device_id=(side, other // nb, lax.rem(other, nb)), device_id_type=MESH
        )

    pl.semaphore_signal(barrier, inc=1, device_id=(1 - side, my_g, my_b), device_id_type=MESH)

    pairs = [
        (diag_hbm, diag),
        (lr_hbm, lr),
        (ur_hbm, ur),
        (ll_hbm, ll),
        (ul_hbm, ul),
        (index_hbm, index),
        (interp_hbm, interp),
        (normals_hbm, normals),
        (areas_hbm, areas),
    ] + [(modes_hbm.at[c], modes.at[:, c * width : (c + 1) * width]) for c in range(3)]
    loads = [pltpu.make_async_copy(a, b, local_sem.at[i]) for i, (a, b) in enumerate(pairs)]
    for load in (loads[5], loads[6], loads[7], *loads[0:5], *loads[9:12], loads[8]):
        load.start()

    for i in (5, 6, 7):
        loads[i].wait()
    rows_pack[...] = jnp.zeros_like(rows_pack)
    rows_pack[0:4, :] = index[...].astype(F32)
    rows_pack[4:8, :] = interp[...]
    rows_pack[8:11, :] = normals[...]
    cols[...] = rows_pack[...].T

    for i in range(5):
        loads[i].wait()
    keep = lax.broadcasted_iota(jnp.int32, (panels, rank_width), 1) < ranks[0]
    lower = jnp.where(keep, ll[...].astype(F32), 0.0).astype(BF16)
    upper = jnp.where(keep, ul[...].astype(F32), 0.0).astype(BF16)
    right = jnp.concatenate([lr[...], ur[...]], axis=1)
    w_high, w_low = split(dot_rows(right, diag[...]))
    wcat[0:two, :] = w_high
    wcat[two : 2 * two, :] = w_low
    both = dot(wcat[...], lower)
    both = both[0:two] + both[two : 2 * two]
    top = dot_rows(ur[...], upper)
    maps[me] = jnp.concatenate(
        [both[0:rank_width], both[rank_width:two], top, jnp.zeros_like(top)], axis=1
    )

    pl.semaphore_wait(barrier, nd)

    def map_copy(k, b):
        return pltpu.make_async_remote_copy(
            src_ref=maps.at[me],
            dst_ref=maps.at[me],
            send_sem=map_send.at[k],
            recv_sem=map_recv.at[k],
            device_id=(side, my_g, b),
            device_id_type=MESH,
        )

    @pl.loop(1, nb)
    def _(k):
        map_copy(k, lax.rem(my_b + k, nb)).start()

    for i in (9, 10, 11):
        loads[i].wait()

    def slab_copy(k, g):
        return pltpu.make_async_remote_copy(
            src_ref=maps.at[pl.ds(my_g * nb, nb)],
            dst_ref=maps.at[pl.ds(my_g * nb, nb)],
            send_sem=slab_send.at[k],
            recv_sem=slab_recv.at[k],
            device_id=(side, g, my_b),
            device_id_type=MESH,
        )

    def vel_copy(kg, kb, g, b):
        return pltpu.make_async_remote_copy(
            src_ref=sendbuf.at[g * nb + b],
            dst_ref=arrived.at[me],
            send_sem=vel_send.at[kg, kb],
            recv_sem=vel_recv.at[kg, kb],
            device_id=(side, g, b),
            device_id_type=MESH,
        )

    chunk = nb * cap
    node_ids = lax.broadcasted_iota(jnp.int32, (TILE, nodes), 1).astype(F32)

    def velocity_chunk(g):
        base = g * chunk

        @pl.loop(0, chunk // TILE, unroll=2)
        def _(i):
            mine = cols[pl.ds(pl.multiple_of(base + i * TILE, TILE), TILE), :]
            total = jnp.zeros((TILE, nodes), F32)
            for k in range(4):
                total += jnp.where(node_ids == mine[:, k : k + 1], mine[:, 4 + k : 5 + k], 0.0)
            wbuf[pl.ds(pl.multiple_of(i * TILE, TILE), TILE), :] = total.astype(BF16)

        moved = dot(wbuf[...], modes[...])
        normal = cols[pl.ds(pl.multiple_of(base, TILE), chunk), :]
        velocity = normal[:, 8:9] * moved[:, 0:width]
        for c in (1, 2):
            velocity += normal[:, 8 + c : 9 + c] * moved[:, c * width : (c + 1) * width]
        sendbuf[pl.ds(g * nb, nb)] = velocity.astype(BF16).reshape(nb, cap, width)

    def velocity_send(kg, g):
        @pl.loop(jnp.where(kg == 0, 1, 0), nb)
        def _(k):
            vel_copy(kg, k, g, lax.rem(my_b + k, nb)).start()

    first = lax.rem(my_g + 1, ng)
    velocity_chunk(first)

    @pl.loop(1, nb)
    def _(k):
        map_copy(k, lax.rem(my_b + k, nb)).wait()

    @pl.loop(1, ng)
    def _(k):
        slab_copy(k, lax.rem(my_g + k, ng)).start()

    velocity_send(lax.rem(jnp.int32(1), ng), first)

    @pl.loop(1, ng)
    def _(step):
        kg = lax.rem(step + 1, ng)
        g = lax.rem(my_g + kg, ng)
        velocity_chunk(g)
        velocity_send(kg, g)

    arrived[me] = sendbuf[me]

    slot_ids = lax.broadcasted_iota(jnp.int32, (1, slots), 1)

    def place(j, carry):
        offset, target = carry
        local = slot_ids - j * cap
        count = counts[j, 0]
        target = jnp.where((local >= 0) & (local < count), local + offset, target)
        return offset + count, target

    _, target = lax.fori_loop(
        0, nd, place, (jnp.int32(0), jnp.full((1, slots), -1, jnp.int32))
    )
    panel_ids = lax.broadcasted_iota(jnp.int32, (TILE, slots), 0)

    @pl.loop(0, panels // TILE, unroll=2)
    def _(i):
        hot = jnp.where(panel_ids + i * TILE == target, 1.0, 0.0)
        pick[pl.ds(pl.multiple_of(i * TILE, TILE), TILE), :] = hot.astype(BF16)

    g_high, g_low = split(dot(diag[...], lower))
    gp[...] = jnp.concatenate([g_high, g_low, g_high, upper, upper], axis=1)

    @pl.loop(1, ng)
    def _(k):
        slab_copy(k, lax.rem(my_g + k, ng)).wait()

    units = ng * two
    row_id = lax.broadcasted_iota(jnp.int32, (rank_width, units), 0)
    col_id = lax.broadcasted_iota(jnp.int32, (rank_width, units), 1)

    def impulse(i, shift):
        gi, bi = i // nb, lax.rem(i, nb)
        hit = jnp.where(bi == my_b, 1.0, 0.0).astype(F32)
        return jnp.where(col_id == row_id + (two * gi + shift), hit, 0.0)

    def three(high, low):
        return jnp.concatenate([high, low, high], axis=1)

    def state(s):
        high, low = split(s)
        return jnp.concatenate([high, high, low], axis=0)

    def forward(i, s):
        high, low = split(maps[i])
        lhs = jnp.concatenate(
            [
                three(high[:, 0:rank_width], low[:, 0:rank_width]),
                three(high[:, rank_width:two], low[:, rank_width:two]),
            ],
            axis=0,
        )

        @pl.when(i // nb == my_g)
        def _():
            kout[lax.rem(i, nb), 0:rank_width, :] = s

        moved = dot(lhs, state(s))
        back_terms[i] = moved[rank_width:two]
        return s - moved[0:rank_width] + impulse(i, 0)

    def backward(step, t):
        i = nd - 1 - step
        high, low = split(maps[i])
        lhs = three(high[:, two : two + rank_width], low[:, two : two + rank_width])

        @pl.when(i // nb == my_g)
        def _():
            kout[lax.rem(i, nb), rank_width:two, :] = t

        return t - dot(lhs, state(t)) + impulse(i, rank_width) - back_terms[i]

    zero = jnp.zeros((rank_width, units), F32)
    lax.fori_loop(0, nd, forward, zero)
    lax.fori_loop(0, nd, backward, zero)

    loads[8].wait()
    area = areas[...].T

    @pl.loop(0, nd - 1)
    def _(k):
        source = k + 1
        vel_copy(source // nb, lax.rem(source, nb), my_g, my_b).wait_recv()

    b = dot(pick[...], arrived[...].reshape(slots, width)).astype(BF16)
    velocities[side] = b
    side_copy = pltpu.make_async_remote_copy(
        src_ref=velocities.at[side],
        dst_ref=velocities.at[side],
        send_sem=side_send,
        recv_sem=side_recv,
        device_id=(1 - side, my_g, my_b),
        device_id_type=MESH,
    )
    z = dot(wcat[...], b)
    zall[my_g] = (z[0:two] + z[two : 2 * two]).astype(BF16)

    def z_copy(k, g):
        return pltpu.make_async_remote_copy(
            src_ref=zall.at[my_g],
            dst_ref=zall.at[my_g],
            send_sem=z_send.at[k],
            recv_sem=z_recv.at[k],
            device_id=(side, g, my_b),
            device_id_type=MESH,
        )

    @pl.loop(1, ng)
    def _(k):
        z_copy(k, lax.rem(my_g + k, ng)).start()

    side_copy.start()
    solved[...] = dot(diag[...], b)

    @pl.loop(1, ng)
    def _(k):
        z_copy(k, lax.rem(my_g + k, ng)).wait()

    k_high, k_low = split(kout[...].reshape(nb * two, units))
    zcat = zall[...].reshape(units, width)
    part = dot(k_high, zcat) + dot(k_low, zcat)
    psend[...] = part.astype(BF16).reshape(nb, two, width)

    def p_copy(k, b):
        return pltpu.make_async_remote_copy(
            src_ref=psend.at[b],
            dst_ref=precv.at[my_b],
            send_sem=p_send.at[k],
            recv_sem=p_recv.at[k],
            device_id=(side, my_g, b),
            device_id_type=MESH,
        )

    @pl.loop(1, nb)
    def _(k):
        p_copy(k, lax.rem(my_b + k, nb)).start()

    precv[my_b] = psend[my_b]
    side_copy.wait()
    for h in range(2):
        velocities_t[h * width : (h + 1) * width, :] = velocities[h].T

    @pl.loop(1, nb)
    def _(k):
        p_copy(k, lax.rem(my_b + k, nb)).wait()

    states = jnp.sum(precv[...].astype(F32), axis=0)
    s_high, s_low = split(states[0:rank_width])
    t_high, t_low = split(states[rank_width:two])
    rhs = jnp.concatenate([s_high, s_high, s_low, t_high, t_low], axis=0)
    potentials = (solved[...] - dot(gp[...], rhs)).astype(BF16)
    pot[...] = potentials
    pot_copy = pltpu.make_async_copy(pot, pot_hbm, local_sem.at[len(pairs)])
    pot_copy.start()
    weighted = (area[:, 0:1] * potentials.astype(F32)).astype(BF16)
    partial = dot(velocities_t[...], weighted).astype(BF16)
    held = msend.shape[1]
    if held != out_rows:
        row = lax.broadcasted_iota(jnp.int32, (nd * held, nd * out_rows), 0)
        col = lax.broadcasted_iota(jnp.int32, (nd * held, nd * out_rows), 1)
        home = (col // out_rows) * held + col % out_rows
        partial = dot(jnp.where(row == home, 1.0, 0.0).astype(BF16), partial).astype(BF16)
    msend[...] = partial.reshape(nd, held, width)

    def m_copy(k, d):
        return pltpu.make_async_remote_copy(
            src_ref=msend.at[d],
            dst_ref=mrecv.at[me],
            send_sem=m_send.at[k],
            recv_sem=m_recv.at[k],
            device_id=(side, d // nb, lax.rem(d, nb)),
            device_id_type=MESH,
        )

    @pl.loop(1, nd)
    def _(k):
        m_copy(k, lax.rem(me + k, nd)).start()

    mrecv[me] = msend[me]

    @pl.loop(0, nd - 1)
    def _(k):
        source = k + 1
        vel_copy(source // nb, lax.rem(source, nb), my_g, my_b).wait_send()

    @pl.loop(1, nd)
    def _(k):
        m_copy(k, lax.rem(me + k, nd)).wait()

    mass_ref[...] = jnp.sum(mrecv[...].astype(F32), axis=0)[0:out_rows]
    pot_copy.wait()


def body(
    node_modes,
    node_index,
    interp,
    normals,
    counts,
    inverse_diag,
    lower_left,
    lower_right,
    upper_left,
    upper_right,
    ranks,
    areas,
):
    ng, nb = lax.axis_size("grp"), lax.axis_size("blk")
    nd = ng * nb
    nodes, width = node_modes.shape[1:]
    cap_given = node_index.shape[1] // nd
    cap = -(-cap_given // TILE) * TILE
    if cap != cap_given:

        def widen(part):
            lead = part.shape[0]
            spare = ((0, 0), (0, 0), (0, cap - cap_given))
            return jnp.pad(part.reshape(lead, nd, cap_given), spare).reshape(lead, nd * cap)

        node_index, interp, normals = widen(node_index), widen(interp), widen(normals)
    slots = nd * cap
    panels = inverse_diag.shape[0]
    rank_width = lower_left.shape[1]
    two = 2 * rank_width
    units = ng * two
    out_rows = 2 * width // nd
    held = -(-out_rows // TILE) * TILE
    areas = areas.reshape(1, panels)
    hbm = pl.BlockSpec(memory_space=pl.ANY)
    smem = pl.BlockSpec(memory_space=pltpu.SMEM)
    vmem = pl.BlockSpec(memory_space=pltpu.VMEM)
    dma = pltpu.SemaphoreType.DMA
    factor = pltpu.VMEM((panels, rank_width), BF16)
    scratch = [
        pltpu.VMEM((nodes, 3 * width), BF16),
        pltpu.VMEM((4, slots), jnp.int32),
        pltpu.VMEM((4, slots), F32),
        pltpu.VMEM((3, slots), F32),
        pltpu.VMEM((panels, panels), BF16),
        factor,
        factor,
        factor,
        factor,
        pltpu.VMEM((1, panels), F32),
        pltpu.VMEM((TILE, slots), F32),
        pltpu.VMEM((slots, TILE), F32),
        pltpu.VMEM((nb * cap, nodes), BF16),
        pltpu.VMEM((nd, cap, width), BF16),
        pltpu.VMEM((nd, cap, width), BF16),
        pltpu.VMEM((panels, slots), BF16),
        pltpu.VMEM((nd, rank_width, 4 * rank_width), F32),
        pltpu.VMEM((nd, rank_width, units), F32),
        pltpu.VMEM((nb, two, units), F32),
        pltpu.VMEM((2 * two, panels), BF16),
        pltpu.VMEM((panels, 5 * rank_width), BF16),
        pltpu.VMEM((panels, width), F32),
        pltpu.VMEM((2, panels, width), BF16),
        pltpu.VMEM((2 * width, panels), BF16),
        pltpu.VMEM((ng, two, width), BF16),
        pltpu.VMEM((nb, two, width), BF16),
        pltpu.VMEM((nb, two, width), BF16),
        pltpu.VMEM((panels, width), BF16),
        pltpu.VMEM((nd, held, width), BF16),
        pltpu.VMEM((nd, held, width), BF16),
        dma((13,)),
        dma((nb,)),
        dma((nb,)),
        dma((ng,)),
        dma((ng,)),
        dma((ng, nb)),
        dma((ng, nb)),
        dma(()),
        dma(()),
        dma((ng,)),
        dma((ng,)),
        dma((nb,)),
        dma((nb,)),
        dma((nd,)),
        dma((nd,)),
    ]
    return pl.pallas_call(
        functools.partial(kernel, ng, nb, cap, out_rows),
        out_shape=(
            jax.ShapeDtypeStruct((panels, width), BF16),
            jax.ShapeDtypeStruct((out_rows, width), F32),
        ),
        in_specs=[hbm, hbm, hbm, hbm, smem, hbm, hbm, hbm, hbm, hbm, smem, hbm],
        out_specs=(hbm, vmem),
        scratch_shapes=scratch,
        compiler_params=pltpu.CompilerParams(
            collective_id=0, has_side_effects=True, vmem_limit_bytes=56 * 1024 * 1024
        ),
    )(
        node_modes,
        node_index,
        interp,
        normals,
        counts,
        inverse_diag,
        lower_left,
        lower_right,
        upper_left,
        upper_right,
        ranks,
        areas,
    )


def solution(mesh):
    split_rows = P(("grp", "blk"), None)
    split_cols = P(None, ("grp", "blk"))
    in_specs = (
        P(None, ("grp", "blk"), "side"),
        split_cols,
        split_cols,
        split_cols,
        split_cols,
        split_rows,
        split_rows,
        split_rows,
        split_rows,
        split_rows,
        P(("grp", "blk")),
        P(("grp", "blk")),
    )
    out_specs = (P(("grp", "blk"), "side"), P(("grp", "blk"), "side"))
    return jax.shard_map(body, mesh=mesh, in_specs=in_specs, out_specs=out_specs, check_vma=False)
```

```python
import functools

import jax
import jax.numpy as jnp
from jax import lax
from jax.experimental import pallas as pl
from jax.experimental.pallas import tpu as pltpu
from jax.sharding import PartitionSpec as P

MESH = pl.DeviceIdType.MESH
F32 = jnp.float32
BF16 = jnp.bfloat16
TILE = 16
LANES = 128


def dot(a, b):
    return jnp.dot(a, b, preferred_element_type=F32)


def dot_rows(a, b):
    return lax.dot_general(a, b, (((0,), (0,)), ((), ())), preferred_element_type=F32)


def dot_lanes(a, b):
    return lax.dot_general(a, b, (((1,), (1,)), ((), ())), preferred_element_type=F32)


def split(a):
    high = a.astype(BF16)
    return high, (a - high.astype(F32)).astype(BF16)


def kernel(
    ng,
    nb,
    cap,
    out_rows,
    modes_hbm,
    index_hbm,
    interp_hbm,
    normals_hbm,
    counts,
    diag_hbm,
    ll_hbm,
    lr_hbm,
    ul_hbm,
    ur_hbm,
    ranks,
    areas_hbm,
    pot_hbm,
    mass_ref,
    modes,
    index,
    interp,
    normals,
    diag,
    ll,
    lr,
    ul,
    ur,
    areas,
    rows_pack,
    cols,
    cols16,
    wbuf,
    sendbuf,
    arrived,
    pick,
    maps,
    left,
    back_terms,
    kout,
    wcat,
    gp,
    solved,
    velocities,
    velocities_t,
    zall,
    psend,
    precv,
    pot,
    msend,
    mrecv,
    local_sem,
    map_send,
    map_recv,
    slab_send,
    slab_recv,
    vel_send,
    vel_recv,
    side_send,
    side_recv,
    z_send,
    z_recv,
    p_send,
    p_recv,
    m_send,
    m_recv,
):
    nd = ng * nb
    rank_width = ll.shape[0]
    two = 2 * rank_width
    panels = diag.shape[0]
    nodes, width3 = modes.shape
    width = width3 // 3
    slots = nd * cap
    side, my_g, my_b = lax.axis_index("side"), lax.axis_index("grp"), lax.axis_index("blk")
    me = my_g * nb + my_b

    barrier = pltpu.get_barrier_semaphore()

    @pl.loop(1, nd)
    def _(k):
        other = lax.rem(me + k, nd)
        pl.semaphore_signal(
            barrier, inc=1, device_id=(side, other // nb, lax.rem(other, nb)), device_id_type=MESH
        )

    pl.semaphore_signal(barrier, inc=1, device_id=(1 - side, my_g, my_b), device_id_type=MESH)

    pairs = [
        (diag_hbm, diag),
        (lr_hbm, lr),
        (ur_hbm, ur),
        (ll_hbm, ll),
        (ul_hbm, ul),
        (index_hbm, index),
        (interp_hbm, interp),
        (normals_hbm, normals),
        (areas_hbm, areas),
    ] + [(modes_hbm.at[c], modes.at[:, c * width : (c + 1) * width]) for c in range(3)]
    loads = [pltpu.make_async_copy(a, b, local_sem.at[i]) for i, (a, b) in enumerate(pairs)]
    for load in (loads[5], loads[6], loads[7], *loads[0:5], *loads[9:12], loads[8]):
        load.start()

    for i in (5, 6, 7):
        loads[i].wait()
    rows_pack[...] = jnp.zeros_like(rows_pack)
    tile_of = index[...] // LANES
    rows_pack[0:4, :] = tile_of.astype(F32)
    rows_pack[4:8, :] = (index[...] - tile_of * LANES).astype(F32)
    rows_pack[8:12, :] = interp[...]
    rows_pack[12:15, :] = normals[...]
    turned = rows_pack[...].T
    cols[...] = turned
    cols16[...] = turned.astype(BF16)

    for i in range(5):
        loads[i].wait()
    keep = lax.broadcasted_iota(jnp.int32, (rank_width, panels), 0) < ranks[0]
    lower = jnp.where(keep, ll[...].astype(F32), 0.0).astype(BF16)
    upper = jnp.where(keep, ul[...].astype(F32), 0.0).astype(BF16)
    right = jnp.concatenate([lr[...], ur[...]], axis=0)
    w_high, w_low = split(dot(right, diag[...]))
    wcat[0:two, :] = w_high
    wcat[two : 2 * two, :] = w_low
    both = dot_lanes(wcat[...], lower)
    both = both[0:two] + both[two : 2 * two]
    top = dot_lanes(ur[...], upper)
    maps[me] = jnp.concatenate(
        [both[0:rank_width], both[rank_width:two], top, jnp.zeros_like(top)], axis=1
    )

    pl.semaphore_wait(barrier, nd)

    def map_copy(k, b):
        return pltpu.make_async_remote_copy(
            src_ref=maps.at[me],
            dst_ref=maps.at[me],
            send_sem=map_send.at[k],
            recv_sem=map_recv.at[k],
            device_id=(side, my_g, b),
            device_id_type=MESH,
        )

    @pl.loop(1, nb)
    def _(k):
        map_copy(k, lax.rem(my_b + k, nb)).start()

    for i in (9, 10, 11):
        loads[i].wait()

    def slab_copy(k, g):
        return pltpu.make_async_remote_copy(
            src_ref=maps.at[pl.ds(my_g * nb, nb)],
            dst_ref=maps.at[pl.ds(my_g * nb, nb)],
            send_sem=slab_send.at[k],
            recv_sem=slab_recv.at[k],
            device_id=(side, g, my_b),
            device_id_type=MESH,
        )

    def vel_copy(kg, kb, g, b):
        return pltpu.make_async_remote_copy(
            src_ref=sendbuf.at[g * nb + b],
            dst_ref=arrived.at[me],
            send_sem=vel_send.at[kg, kb],
            recv_sem=vel_recv.at[kg, kb],
            device_id=(side, g, b),
            device_id_type=MESH,
        )

    chunk = nb * cap
    lane_ids = lax.broadcasted_iota(jnp.int32, (TILE, LANES), 1).astype(F32).astype(BF16)
    zero16 = jnp.zeros((TILE, LANES), BF16)

    def velocity_chunk(g):
        base = g * chunk

        @pl.loop(0, chunk // TILE, unroll=2)
        def _(i):
            mine = cols16[pl.ds(pl.multiple_of(base + i * TILE, TILE), TILE), :]
            wide = [jnp.broadcast_to(mine[:, c : c + 1], (TILE, LANES)) for c in range(12)]
            lit = [jnp.where(lane_ids == wide[4 + k], wide[8 + k], zero16) for k in range(4)]
            for tile in range(nodes // LANES):
                terms = [jnp.where(wide[k] == jnp.asarray(tile, BF16), lit[k], zero16) for k in range(4)]
                total = (terms[0] + terms[1]) + (terms[2] + terms[3])
                wbuf[
                    pl.ds(pl.multiple_of(i * TILE, TILE), TILE), tile * LANES : (tile + 1) * LANES
                ] = total

        moved = dot(wbuf[...], modes[...])
        normal = cols[pl.ds(pl.multiple_of(base, TILE), chunk), :]
        velocity = normal[:, 12:13] * moved[:, 0:width]
        for c in (1, 2):
            velocity += normal[:, 12 + c : 13 + c] * moved[:, c * width : (c + 1) * width]
        sendbuf[pl.ds(g * nb, nb)] = velocity.astype(BF16).reshape(nb, cap, width)

    def velocity_send(kg, g):
        @pl.loop(jnp.where(kg == 0, 1, 0), nb)
        def _(k):
            vel_copy(kg, k, g, lax.rem(my_b + k, nb)).start()

    first = lax.rem(my_g + 1, ng)
    velocity_chunk(first)

    @pl.loop(1, nb)
    def _(k):
        map_copy(k, lax.rem(my_b + k, nb)).wait()

    @pl.loop(1, ng)
    def _(k):
        slab_copy(k, lax.rem(my_g + k, ng)).start()

    velocity_send(lax.rem(jnp.int32(1), ng), first)

    @pl.loop(1, ng)
    def _(step):
        kg = lax.rem(step + 1, ng)
        g = lax.rem(my_g + kg, ng)
        velocity_chunk(g)
        velocity_send(kg, g)

    arrived[me] = sendbuf[me]

    slot_ids = lax.broadcasted_iota(jnp.int32, (1, slots), 1)

    def place(j, carry):
        offset, target = carry
        local = slot_ids - j * cap
        count = counts[0, j]
        target = jnp.where((local >= 0) & (local < count), local + offset, target)
        return offset + count, target

    _, target = lax.fori_loop(
        0, nd, place, (jnp.int32(0), jnp.full((1, slots), -1, jnp.int32))
    )
    panel_ids = lax.broadcasted_iota(jnp.int32, (TILE, slots), 0)

    @pl.loop(0, panels // TILE, unroll=2)
    def _(i):
        hot = jnp.where(panel_ids + i * TILE == target, 1.0, 0.0)
        pick[pl.ds(pl.multiple_of(i * TILE, TILE), TILE), :] = hot.astype(BF16)

    g_high, g_low = split(dot_lanes(lower, diag[...]))
    gp[...] = jnp.concatenate([g_high, g_low, g_high, upper, upper], axis=0).T

    @pl.loop(1, ng)
    def _(k):
        slab_copy(k, lax.rem(my_g + k, ng)).wait()

    units = ng * two
    row_id = lax.broadcasted_iota(jnp.int32, (rank_width, units), 0)
    col_id = lax.broadcasted_iota(jnp.int32, (rank_width, units), 1)

    def impulse(i, shift):
        gi, bi = i // nb, lax.rem(i, nb)
        hit = jnp.where(bi == my_b, 1.0, 0.0).astype(F32)
        return jnp.where(col_id == row_id + (two * gi + shift), hit, 0.0)

    def three(high, low):
        return jnp.concatenate([high, low, high], axis=1)

    def state(s):
        high, low = split(s)
        return jnp.concatenate([high, high, low], axis=0)

    three_wide = 3 * rank_width

    @pl.loop(0, nd, unroll=2)
    def _(i):
        high, low = split(maps[i])
        for c in range(3):
            span = slice(c * rank_width, (c + 1) * rank_width)
            left[i, span, :] = three(high[:, span], low[:, span])

    def forward(i, s):
        @pl.when(i // nb == my_g)
        def _():
            kout[lax.rem(i, nb), 0:rank_width, :] = s

        moved = dot(left[i, 0:two, :], state(s))
        back_terms[i] = moved[rank_width:two]
        return s - moved[0:rank_width] + impulse(i, 0)

    def backward(step, t):
        i = nd - 1 - step

        @pl.when(i // nb == my_g)
        def _():
            kout[lax.rem(i, nb), rank_width:two, :] = t

        base = t + (impulse(i, rank_width) - back_terms[i])
        return base - dot(left[i, two:three_wide, :], state(t))

    zero = jnp.zeros((rank_width, units), F32)
    lax.fori_loop(0, nd, forward, zero)
    lax.fori_loop(0, nd, backward, zero)

    loads[8].wait()
    area = areas[...].T

    @pl.loop(0, nd - 1)
    def _(k):
        source = k + 1
        vel_copy(source // nb, lax.rem(source, nb), my_g, my_b).wait_recv()

    b = dot(pick[...], arrived[...].reshape(slots, width)).astype(BF16)
    velocities[side] = b
    side_copy = pltpu.make_async_remote_copy(
        src_ref=velocities.at[side],
        dst_ref=velocities.at[side],
        send_sem=side_send,
        recv_sem=side_recv,
        device_id=(1 - side, my_g, my_b),
        device_id_type=MESH,
    )
    z = dot(wcat[...], b)
    zall[my_g] = (z[0:two] + z[two : 2 * two]).astype(BF16)

    def z_copy(k, g):
        return pltpu.make_async_remote_copy(
            src_ref=zall.at[my_g],
            dst_ref=zall.at[my_g],
            send_sem=z_send.at[k],
            recv_sem=z_recv.at[k],
            device_id=(side, g, my_b),
            device_id_type=MESH,
        )

    @pl.loop(1, ng)
    def _(k):
        z_copy(k, lax.rem(my_g + k, ng)).start()

    side_copy.start()
    solved[...] = dot(diag[...], b)

    @pl.loop(1, ng)
    def _(k):
        z_copy(k, lax.rem(my_g + k, ng)).wait()

    k_high, k_low = split(kout[...].reshape(nb * two, units))
    zcat = zall[...].reshape(units, width)
    part = dot(k_high, zcat) + dot(k_low, zcat)
    psend[...] = part.astype(BF16).reshape(nb, two, width)

    def p_copy(k, b):
        return pltpu.make_async_remote_copy(
            src_ref=psend.at[b],
            dst_ref=precv.at[my_b],
            send_sem=p_send.at[k],
            recv_sem=p_recv.at[k],
            device_id=(side, my_g, b),
            device_id_type=MESH,
        )

    @pl.loop(1, nb)
    def _(k):
        p_copy(k, lax.rem(my_b + k, nb)).start()

    precv[my_b] = psend[my_b]
    side_copy.wait()
    for h in range(2):
        velocities_t[h * width : (h + 1) * width, :] = velocities[h].T

    @pl.loop(1, nb)
    def _(k):
        p_copy(k, lax.rem(my_b + k, nb)).wait()

    states = jnp.sum(precv[...].astype(F32), axis=0)
    s_high, s_low = split(states[0:rank_width])
    t_high, t_low = split(states[rank_width:two])
    rhs = jnp.concatenate([s_high, s_high, s_low, t_high, t_low], axis=0)
    potentials = (solved[...] - dot(gp[...], rhs)).astype(BF16)
    pot[...] = potentials
    pot_copy = pltpu.make_async_copy(pot, pot_hbm, local_sem.at[len(pairs)])
    pot_copy.start()
    weighted = (area[:, 0:1] * potentials.astype(F32)).astype(BF16)
    partial = dot(velocities_t[...], weighted).astype(BF16)
    held = msend.shape[1]
    if held != out_rows:
        row = lax.broadcasted_iota(jnp.int32, (nd * held, nd * out_rows), 0)
        col = lax.broadcasted_iota(jnp.int32, (nd * held, nd * out_rows), 1)
        home = (col // out_rows) * held + col % out_rows
        partial = dot(jnp.where(row == home, 1.0, 0.0).astype(BF16), partial).astype(BF16)
    msend[...] = partial.reshape(nd, held, width)

    def m_copy(k, d):
        return pltpu.make_async_remote_copy(
            src_ref=msend.at[d],
            dst_ref=mrecv.at[me],
            send_sem=m_send.at[k],
            recv_sem=m_recv.at[k],
            device_id=(side, d // nb, lax.rem(d, nb)),
            device_id_type=MESH,
        )

    @pl.loop(1, nd)
    def _(k):
        m_copy(k, lax.rem(me + k, nd)).start()

    mrecv[me] = msend[me]

    @pl.loop(0, nd - 1)
    def _(k):
        source = k + 1
        vel_copy(source // nb, lax.rem(source, nb), my_g, my_b).wait_send()

    @pl.loop(1, nd)
    def _(k):
        m_copy(k, lax.rem(me + k, nd)).wait()

    mass_ref[...] = jnp.sum(mrecv[...].astype(F32), axis=0)[0:out_rows]
    pot_copy.wait()


def hand_over(pot_in, mass_in, pot_out, mass_out, sem):
    copy = pltpu.make_async_copy(pot_in, pot_out, sem)
    copy.start()
    mass_out[...] = mass_in[...]
    copy.wait()


def body(
    node_modes,
    node_index,
    interp,
    normals,
    counts,
    inverse_diag,
    lower_left,
    lower_right,
    upper_left,
    upper_right,
    ranks,
    areas,
):
    ng, nb = lax.axis_size("grp"), lax.axis_size("blk")
    nd = ng * nb
    nodes, width = node_modes.shape[1:]
    cap_given = node_index.shape[1] // nd
    cap = -(-cap_given // TILE) * TILE
    if cap != cap_given:

        def widen(part):
            lead = part.shape[0]
            spare = ((0, 0), (0, 0), (0, cap - cap_given))
            return jnp.pad(part.reshape(lead, nd, cap_given), spare).reshape(lead, nd * cap)

        node_index, interp, normals = widen(node_index), widen(interp), widen(normals)
    slots = nd * cap
    panels = inverse_diag.shape[0]
    rank_width = lower_left.shape[1]
    factors = [part.T for part in (lower_left, lower_right, upper_left, upper_right)]
    two = 2 * rank_width
    units = ng * two
    out_rows = 2 * width // nd
    held = -(-out_rows // TILE) * TILE
    areas = areas.reshape(1, panels)
    shapes = (
        jax.ShapeDtypeStruct((panels, width), BF16),
        jax.ShapeDtypeStruct((out_rows, width), F32),
    )
    hbm = pl.BlockSpec(memory_space=pl.ANY)
    smem = pl.BlockSpec(memory_space=pltpu.SMEM)
    vmem = pl.BlockSpec(memory_space=pltpu.VMEM)
    dma = pltpu.SemaphoreType.DMA
    factor = pltpu.VMEM((rank_width, panels), BF16)
    scratch = [
        pltpu.VMEM((nodes, 3 * width), BF16),
        pltpu.VMEM((4, slots), jnp.int32),
        pltpu.VMEM((4, slots), F32),
        pltpu.VMEM((3, slots), F32),
        pltpu.VMEM((panels, panels), BF16),
        factor,
        factor,
        factor,
        factor,
        pltpu.VMEM((1, panels), F32),
        pltpu.VMEM((TILE, slots), F32),
        pltpu.VMEM((slots, TILE), F32),
        pltpu.VMEM((slots, TILE), BF16),
        pltpu.VMEM((nb * cap, nodes), BF16),
        pltpu.VMEM((nd, cap, width), BF16),
        pltpu.VMEM((nd, cap, width), BF16),
        pltpu.VMEM((panels, slots), BF16),
        pltpu.VMEM((nd, rank_width, 4 * rank_width), F32),
        pltpu.VMEM((nd, 3 * rank_width, 3 * rank_width), BF16),
        pltpu.VMEM((nd, rank_width, units), F32),
        pltpu.VMEM((nb, two, units), F32),
        pltpu.VMEM((2 * two, panels), BF16),
        pltpu.VMEM((panels, 5 * rank_width), BF16),
        pltpu.VMEM((panels, width), F32),
        pltpu.VMEM((2, panels, width), BF16),
        pltpu.VMEM((2 * width, panels), BF16),
        pltpu.VMEM((ng, two, width), BF16),
        pltpu.VMEM((nb, two, width), BF16),
        pltpu.VMEM((nb, two, width), BF16),
        pltpu.VMEM((panels, width), BF16),
        pltpu.VMEM((nd, held, width), BF16),
        pltpu.VMEM((nd, held, width), BF16),
        dma((13,)),
        dma((nb,)),
        dma((nb,)),
        dma((ng,)),
        dma((ng,)),
        dma((ng, nb)),
        dma((ng, nb)),
        dma(()),
        dma(()),
        dma((ng,)),
        dma((ng,)),
        dma((nb,)),
        dma((nb,)),
        dma((nd,)),
        dma((nd,)),
    ]
    potentials, mass = pl.pallas_call(
        functools.partial(kernel, ng, nb, cap, out_rows),
        out_shape=shapes,
        in_specs=[hbm, hbm, hbm, hbm, smem, hbm, hbm, hbm, hbm, hbm, smem, hbm],
        out_specs=(hbm, vmem),
        scratch_shapes=scratch,
        compiler_params=pltpu.CompilerParams(
            collective_id=0, has_side_effects=True, vmem_limit_bytes=56 * 1024 * 1024
        ),
    )(
        node_modes,
        node_index,
        interp,
        normals,
        counts.reshape(1, nd),
        inverse_diag,
        *factors,
        ranks,
        areas,
    )
    return pl.pallas_call(
        hand_over,
        out_shape=shapes,
        in_specs=[hbm, vmem],
        out_specs=(hbm, vmem),
        scratch_shapes=[dma(())],
        compiler_params=pltpu.CompilerParams(vmem_limit_bytes=56 * 1024 * 1024),
    )(potentials, mass)


def solution(mesh):
    split_rows = P(("grp", "blk"), None)
    split_cols = P(None, ("grp", "blk"))
    in_specs = (
        P(None, ("grp", "blk"), "side"),
        split_cols,
        split_cols,
        split_cols,
        split_cols,
        split_rows,
        split_rows,
        split_rows,
        split_rows,
        split_rows,
        P(("grp", "blk")),
        P(("grp", "blk")),
    )
    out_specs = (P(("grp", "blk"), "side"), P(("grp", "blk"), "side"))
    return jax.shard_map(body, mesh=mesh, in_specs=in_specs, out_specs=out_specs, check_vma=False)
```

```python
import functools

import jax
import jax.numpy as jnp
from jax import lax
from jax.experimental import pallas as pl
from jax.experimental.pallas import tpu as pltpu
from jax.sharding import PartitionSpec as P

MESH = pl.DeviceIdType.MESH
F32 = jnp.float32
BF16 = jnp.bfloat16
TILE = 16
LANES = 128


def dot(a, b):
    return jnp.dot(a, b, preferred_element_type=F32)


def dot_rows(a, b):
    return lax.dot_general(a, b, (((0,), (0,)), ((), ())), preferred_element_type=F32)


def dot_lanes(a, b):
    return lax.dot_general(a, b, (((1,), (1,)), ((), ())), preferred_element_type=F32)


def split(a):
    high = a.astype(BF16)
    return high, (a - high.astype(F32)).astype(BF16)


def kernel(
    ng,
    nb,
    cap,
    out_rows,
    modes_hbm,
    index_hbm,
    interp_hbm,
    normals_hbm,
    counts,
    diag_hbm,
    ll_hbm,
    lr_hbm,
    ul_hbm,
    ur_hbm,
    ranks,
    areas_hbm,
    pot_hbm,
    mass_ref,
    modes,
    index,
    interp,
    normals,
    diag,
    ll,
    lr,
    ul,
    ur,
    areas,
    rows_pack,
    cols,
    cols16,
    wbuf,
    sendbuf,
    arrived,
    pick,
    maps,
    left,
    record,
    back_terms,
    kout,
    wcat,
    gp,
    bu,
    solved,
    velocities,
    velocities_t,
    zall,
    psend,
    precv,
    pot,
    msend,
    mrecv,
    local_sem,
    map_send,
    map_recv,
    slab_send,
    slab_recv,
    vel_send,
    vel_recv,
    side_send,
    side_recv,
    z_send,
    z_recv,
    p_send,
    p_recv,
    m_send,
    m_recv,
):
    nd = ng * nb
    rank_width = ll.shape[0]
    two = 2 * rank_width
    panels = diag.shape[0]
    nodes, width3 = modes.shape
    width = width3 // 3
    slots = nd * cap
    side, my_g, my_b = lax.axis_index("side"), lax.axis_index("grp"), lax.axis_index("blk")
    me = my_g * nb + my_b

    barrier = pltpu.get_barrier_semaphore()

    @pl.loop(1, nd)
    def _(k):
        other = lax.rem(me + k, nd)
        pl.semaphore_signal(
            barrier, inc=1, device_id=(side, other // nb, lax.rem(other, nb)), device_id_type=MESH
        )

    pl.semaphore_signal(barrier, inc=1, device_id=(1 - side, my_g, my_b), device_id_type=MESH)

    pairs = [
        (diag_hbm, diag),
        (lr_hbm, lr),
        (ur_hbm, ur),
        (ll_hbm, ll),
        (ul_hbm, ul),
        (index_hbm, index),
        (interp_hbm, interp),
        (normals_hbm, normals),
        (areas_hbm, areas),
    ] + [(modes_hbm.at[c], modes.at[:, c * width : (c + 1) * width]) for c in range(3)]
    loads = [pltpu.make_async_copy(a, b, local_sem.at[i]) for i, (a, b) in enumerate(pairs)]
    for load in (*loads[5:8], *loads[9:12], *loads[0:5], loads[8]):
        load.start()

    for i in (5, 6, 7):
        loads[i].wait()
    rows_pack[...] = jnp.zeros_like(rows_pack)
    tile_of = index[...] // LANES
    rows_pack[0:4, :] = tile_of.astype(F32)
    rows_pack[4:8, :] = (index[...] - tile_of * LANES).astype(F32)
    rows_pack[8:12, :] = interp[...]
    rows_pack[12:15, :] = normals[...]
    turned = rows_pack[...].T
    cols[...] = turned
    cols16[...] = turned.astype(BF16)

    def map_copy(k, b):
        return pltpu.make_async_remote_copy(
            src_ref=maps.at[me],
            dst_ref=maps.at[me],
            send_sem=map_send.at[k],
            recv_sem=map_recv.at[k],
            device_id=(side, my_g, b),
            device_id_type=MESH,
        )

    for i in (9, 10, 11):
        loads[i].wait()

    def slab_copy(k, g):
        return pltpu.make_async_remote_copy(
            src_ref=maps.at[pl.ds(my_g * nb, nb)],
            dst_ref=maps.at[pl.ds(my_g * nb, nb)],
            send_sem=slab_send.at[k],
            recv_sem=slab_recv.at[k],
            device_id=(side, g, my_b),
            device_id_type=MESH,
        )

    def vel_copy(kg, kb, g, b):
        return pltpu.make_async_remote_copy(
            src_ref=sendbuf.at[g * nb + b],
            dst_ref=arrived.at[me],
            send_sem=vel_send.at[kg, kb],
            recv_sem=vel_recv.at[kg, kb],
            device_id=(side, g, b),
            device_id_type=MESH,
        )

    chunk = nb * cap
    lane_ids = lax.broadcasted_iota(jnp.int32, (TILE, LANES), 1).astype(F32).astype(BF16)
    zero16 = jnp.zeros((TILE, LANES), BF16)

    def velocity_chunk(g):
        base = g * chunk

        @pl.loop(0, chunk // TILE, unroll=2)
        def _(i):
            mine = cols16[pl.ds(pl.multiple_of(base + i * TILE, TILE), TILE), :]
            wide = [jnp.broadcast_to(mine[:, c : c + 1], (TILE, LANES)) for c in range(12)]
            lit = [jnp.where(lane_ids == wide[4 + k], wide[8 + k], zero16) for k in range(4)]
            for tile in range(nodes // LANES):
                terms = [jnp.where(wide[k] == jnp.asarray(tile, BF16), lit[k], zero16) for k in range(4)]
                total = (terms[0] + terms[1]) + (terms[2] + terms[3])
                wbuf[
                    pl.ds(pl.multiple_of(i * TILE, TILE), TILE), tile * LANES : (tile + 1) * LANES
                ] = total

        moved = dot(wbuf[...], modes[...])
        normal = cols[pl.ds(pl.multiple_of(base, TILE), chunk), :]
        velocity = normal[:, 12:13] * moved[:, 0:width]
        for c in (1, 2):
            velocity += normal[:, 12 + c : 13 + c] * moved[:, c * width : (c + 1) * width]
        sendbuf[pl.ds(g * nb, nb)] = velocity.astype(BF16).reshape(nb, cap, width)

    def velocity_send(kg, g):
        @pl.loop(jnp.where(kg == 0, 1, 0), nb)
        def _(k):
            vel_copy(kg, k, g, lax.rem(my_b + k, nb)).start()

    first = lax.rem(my_g + 1, ng)
    velocity_chunk(first)
    pl.semaphore_wait(barrier, nd)
    velocity_send(lax.rem(jnp.int32(1), ng), first)

    for i in range(5):
        loads[i].wait()
    keep = lax.broadcasted_iota(jnp.int32, (rank_width, panels), 0) < ranks[0]
    lower = jnp.where(keep, ll[...].astype(F32), 0.0).astype(BF16)
    upper = jnp.where(keep, ul[...].astype(F32), 0.0).astype(BF16)
    right = jnp.concatenate([lr[...], ur[...]], axis=0)
    w_high, w_low = split(dot(right, diag[...]))
    wcat[0:two, :] = w_high
    wcat[two : 2 * two, :] = w_low
    both = dot_lanes(wcat[...], lower)
    both = both[0:two] + both[two : 2 * two]
    top = dot_lanes(ur[...], upper)
    maps[me] = jnp.concatenate(
        [both[0:rank_width], both[rank_width:two], top, jnp.zeros_like(top)], axis=1
    )

    @pl.loop(1, nb)
    def _(k):
        map_copy(k, lax.rem(my_b + k, nb)).start()

    lower_t = lower.astype(F32).T.astype(BF16)
    upper_t = upper.astype(F32).T.astype(BF16)
    bu[:, width : width + rank_width] = lower_t
    gp[:, 3 * rank_width : 4 * rank_width] = upper_t
    gp[:, 4 * rank_width : 5 * rank_width] = upper_t

    def rest(step):
        kg = lax.rem(step + 1, ng)
        g = lax.rem(my_g + kg, ng)
        velocity_chunk(g)
        velocity_send(kg, g)

    rest(jnp.int32(1))

    @pl.loop(1, nb)
    def _(k):
        map_copy(k, lax.rem(my_b + k, nb)).wait()

    @pl.loop(1, ng)
    def _(k):
        slab_copy(k, lax.rem(my_g + k, ng)).start()

    pl.loop(2, ng)(rest)

    arrived[me] = sendbuf[me]

    slot_ids = lax.broadcasted_iota(jnp.int32, (1, slots), 1)

    def place(j, carry):
        offset, target = carry
        local = slot_ids - j * cap
        count = counts[0, j]
        target = jnp.where((local >= 0) & (local < count), local + offset, target)
        return offset + count, target

    _, target = lax.fori_loop(
        0, nd, place, (jnp.int32(0), jnp.full((1, slots), -1, jnp.int32))
    )
    panel_ids = lax.broadcasted_iota(jnp.int32, (TILE, slots), 0)

    per_step = panels // TILE // (2 * nb)

    def pick_rows(step):
        for r in range(per_step):
            i = step * per_step + r
            hot = jnp.where(panel_ids + i * TILE == target, 1.0, 0.0)
            pick[pl.ds(pl.multiple_of(i * TILE, TILE), TILE), :] = hot.astype(BF16)

    @pl.loop(1, ng)
    def _(k):
        slab_copy(k, lax.rem(my_g + k, ng)).wait()

    units = ng * two
    span = 4 * rank_width

    def three(high, low):
        return jnp.concatenate([high, low, high], axis=1)

    def state(s):
        high, low = split(s)
        return jnp.concatenate([high, high, low], axis=0)

    @pl.loop(0, nd, unroll=4)
    def _(i):
        high, low = split(maps[i])
        for c in range(3):
            part = slice(c * rank_width, (c + 1) * rank_width)
            left[i, part, :] = three(high[:, part], low[:, part])

    row_id = lax.broadcasted_iota(jnp.int32, (rank_width, span), 0)
    col_id = lax.broadcasted_iota(jnp.int32, (rank_width, span), 1)

    def unit(place):
        return jnp.where(col_id == row_id + place * rank_width, 1.0, 0.0)

    def forward(b, states):
        hit = jnp.where(b == my_b, 1.0, 0.0)
        after = []
        for g in range(ng):
            i = g * nb + b
            record[i, 0:rank_width, :] = states[g]
            moved = dot(left[i, 0:two, :], state(states[g]))
            back_terms[i] = moved[rank_width:two]
            after.append(states[g] - moved[0:rank_width] + hit * unit(2))
        pick_rows(b)
        return tuple(after)

    def backward(step, states):
        b = nb - 1 - step
        hit = jnp.where(b == my_b, 1.0, 0.0)
        after = []
        for g in range(ng):
            i = g * nb + b
            record[i, rank_width:two, :] = states[g]
            moved = dot(left[i, two : 3 * rank_width, :], state(states[g]))
            after.append(states[g] + (hit * unit(3) - back_terms[i]) - moved)
        pick_rows(nb + step)
        return tuple(after)

    ahead = lax.fori_loop(0, nb, forward, (unit(1),) * ng)
    behind = lax.fori_loop(0, nb, backward, (unit(0),) * ng)

    row_two = lax.broadcasted_iota(jnp.int32, (two, units), 0)
    col_two = lax.broadcasted_iota(jnp.int32, (two, units), 1)

    def terms_of(g):
        return jnp.where(col_two == row_two + two * g, 1.0, 0.0).astype(BF16)

    nothing = jnp.zeros((rank_width, units), F32)

    def across(lhs, t, s, g):
        l_high, l_low = split(lhs)
        t_high, t_low = split(t)
        s_high, s_low = split(s)
        own = terms_of(g)
        high = jnp.concatenate([t_high, s_high, own], axis=0)
        low = jnp.concatenate([t_low, s_low, jnp.zeros_like(own)], axis=0)
        return dot(l_high, high) + dot(l_low, high) + dot(l_high, low)

    s_in, t_in = [nothing], [nothing]
    for g in range(ng - 1):
        s_in.append(across(ahead[g], nothing, s_in[g], g))
    for g in range(ng - 1, 0, -1):
        t_in.append(across(behind[g], t_in[-1], s_in[g], g))
    t_in = t_in[::-1]
    s_here, t_here = nothing, nothing
    for g in range(ng):
        s_here = jnp.where(my_g == g, s_in[g], s_here)
        t_here = jnp.where(my_g == g, t_in[g], t_here)
    mine = record[pl.ds(my_g * nb, nb)].reshape(nb * two, span)
    k_high, k_low = split(across(mine, t_here, s_here, my_g))
    kout[:, 0:units] = k_high
    kout[:, units : 2 * units] = k_low

    loads[8].wait()
    area = areas[...].T

    @pl.loop(0, nd - 1)
    def _(k):
        source = k + 1
        vel_copy(source // nb, lax.rem(source, nb), my_g, my_b).wait_recv()

    b = dot(pick[...], arrived[...].reshape(slots, width)).astype(BF16)
    velocities[side] = b
    side_copy = pltpu.make_async_remote_copy(
        src_ref=velocities.at[side],
        dst_ref=velocities.at[side],
        send_sem=side_send,
        recv_sem=side_recv,
        device_id=(1 - side, my_g, my_b),
        device_id_type=MESH,
    )
    z = dot(wcat[...], b)
    zall[my_g] = (z[0:two] + z[two : 2 * two]).astype(BF16)

    def z_copy(k, g):
        return pltpu.make_async_remote_copy(
            src_ref=zall.at[my_g],
            dst_ref=zall.at[my_g],
            send_sem=z_send.at[k],
            recv_sem=z_recv.at[k],
            device_id=(side, g, my_b),
            device_id_type=MESH,
        )

    @pl.loop(1, ng)
    def _(k):
        z_copy(k, lax.rem(my_g + k, ng)).start()

    side_copy.start()
    bu[:, 0:width] = b
    both = dot(diag[...], bu[...])
    solved[...] = both[:, 0:width]
    g_high, g_low = split(both[:, width : width + rank_width])
    gp[:, 0:rank_width] = g_high
    gp[:, rank_width:two] = g_low
    gp[:, two : 3 * rank_width] = g_high

    @pl.loop(1, ng)
    def _(k):
        z_copy(k, lax.rem(my_g + k, ng)).wait()

    zcat = zall[...].reshape(units, width)
    part = dot(kout[...], jnp.concatenate([zcat, zcat], axis=0))
    psend[...] = part.astype(BF16).reshape(nb, two, width)

    def p_copy(k, b):
        return pltpu.make_async_remote_copy(
            src_ref=psend.at[b],
            dst_ref=precv.at[my_b],
            send_sem=p_send.at[k],
            recv_sem=p_recv.at[k],
            device_id=(side, my_g, b),
            device_id_type=MESH,
        )

    @pl.loop(1, nb)
    def _(k):
        p_copy(k, lax.rem(my_b + k, nb)).start()

    precv[my_b] = psend[my_b]
    side_copy.wait()
    for h in range(2):
        velocities_t[h * width : (h + 1) * width, :] = velocities[h].T

    @pl.loop(1, nb)
    def _(k):
        p_copy(k, lax.rem(my_b + k, nb)).wait()

    states = jnp.sum(precv[...].astype(F32), axis=0)
    s_high, s_low = split(states[0:rank_width])
    t_high, t_low = split(states[rank_width:two])
    rhs = jnp.concatenate([s_high, s_high, s_low, t_high, t_low], axis=0)
    potentials = (solved[...] - dot(gp[...], rhs)).astype(BF16)
    pot[...] = potentials
    pot_copy = pltpu.make_async_copy(pot, pot_hbm, local_sem.at[len(pairs)])
    pot_copy.start()
    weighted = (area[:, 0:1] * potentials.astype(F32)).astype(BF16)
    partial = dot(velocities_t[...], weighted).astype(BF16)
    held = msend.shape[1]
    if held != out_rows:
        row = lax.broadcasted_iota(jnp.int32, (nd * held, nd * out_rows), 0)
        col = lax.broadcasted_iota(jnp.int32, (nd * held, nd * out_rows), 1)
        home = (col // out_rows) * held + col % out_rows
        partial = dot(jnp.where(row == home, 1.0, 0.0).astype(BF16), partial).astype(BF16)
    msend[...] = partial.reshape(nd, held, width)

    def m_copy(k, d):
        return pltpu.make_async_remote_copy(
            src_ref=msend.at[d],
            dst_ref=mrecv.at[me],
            send_sem=m_send.at[k],
            recv_sem=m_recv.at[k],
            device_id=(side, d // nb, lax.rem(d, nb)),
            device_id_type=MESH,
        )

    @pl.loop(1, nd)
    def _(k):
        m_copy(k, lax.rem(me + k, nd)).start()

    mrecv[me] = msend[me]

    @pl.loop(0, nd - 1)
    def _(k):
        source = k + 1
        vel_copy(source // nb, lax.rem(source, nb), my_g, my_b).wait_send()

    @pl.loop(1, nd)
    def _(k):
        m_copy(k, lax.rem(me + k, nd)).wait()

    mass_ref[...] = jnp.sum(mrecv[...].astype(F32), axis=0)[0:out_rows]
    pot_copy.wait()


def hand_over(pot_in, mass_in, pot_out, mass_out, sem):
    copy = pltpu.make_async_copy(pot_in, pot_out, sem)
    copy.start()
    mass_out[...] = mass_in[...]
    copy.wait()


def body(
    node_modes,
    node_index,
    interp,
    normals,
    counts,
    inverse_diag,
    lower_left,
    lower_right,
    upper_left,
    upper_right,
    ranks,
    areas,
):
    ng, nb = lax.axis_size("grp"), lax.axis_size("blk")
    nd = ng * nb
    nodes, width = node_modes.shape[1:]
    cap_given = node_index.shape[1] // nd
    cap = -(-cap_given // TILE) * TILE
    if cap != cap_given:

        def widen(part):
            lead = part.shape[0]
            spare = ((0, 0), (0, 0), (0, cap - cap_given))
            return jnp.pad(part.reshape(lead, nd, cap_given), spare).reshape(lead, nd * cap)

        node_index, interp, normals = widen(node_index), widen(interp), widen(normals)
    slots = nd * cap
    panels = inverse_diag.shape[0]
    rank_width = lower_left.shape[1]
    factors = [part.T for part in (lower_left, lower_right, upper_left, upper_right)]
    two = 2 * rank_width
    units = ng * two
    out_rows = 2 * width // nd
    held = -(-out_rows // TILE) * TILE
    areas = areas.reshape(1, panels)
    shapes = (
        jax.ShapeDtypeStruct((panels, width), BF16),
        jax.ShapeDtypeStruct((out_rows, width), F32),
    )
    hbm = pl.BlockSpec(memory_space=pl.ANY)
    smem = pl.BlockSpec(memory_space=pltpu.SMEM)
    vmem = pl.BlockSpec(memory_space=pltpu.VMEM)
    dma = pltpu.SemaphoreType.DMA
    factor = pltpu.VMEM((rank_width, panels), BF16)
    scratch = [
        pltpu.VMEM((nodes, 3 * width), BF16),
        pltpu.VMEM((4, slots), jnp.int32),
        pltpu.VMEM((4, slots), F32),
        pltpu.VMEM((3, slots), F32),
        pltpu.VMEM((panels, panels), BF16),
        factor,
        factor,
        factor,
        factor,
        pltpu.VMEM((1, panels), F32),
        pltpu.VMEM((TILE, slots), F32),
        pltpu.VMEM((slots, TILE), F32),
        pltpu.VMEM((slots, TILE), BF16),
        pltpu.VMEM((nb * cap, nodes), BF16),
        pltpu.VMEM((nd, cap, width), BF16),
        pltpu.VMEM((nd, cap, width), BF16),
        pltpu.VMEM((panels, slots), BF16),
        pltpu.VMEM((nd, rank_width, 4 * rank_width), F32),
        pltpu.VMEM((nd, 3 * rank_width, 3 * rank_width), BF16),
        pltpu.VMEM((nd, two, 4 * rank_width), F32),
        pltpu.VMEM((nd, rank_width, 4 * rank_width), F32),
        pltpu.VMEM((nb * two, 2 * units), BF16),
        pltpu.VMEM((2 * two, panels), BF16),
        pltpu.VMEM((panels, 5 * rank_width), BF16),
        pltpu.VMEM((panels, width + rank_width), BF16),
        pltpu.VMEM((panels, width), F32),
        pltpu.VMEM((2, panels, width), BF16),
        pltpu.VMEM((2 * width, panels), BF16),
        pltpu.VMEM((ng, two, width), BF16),
        pltpu.VMEM((nb, two, width), BF16),
        pltpu.VMEM((nb, two, width), BF16),
        pltpu.VMEM((panels, width), BF16),
        pltpu.VMEM((nd, held, width), BF16),
        pltpu.VMEM((nd, held, width), BF16),
        dma((13,)),
        dma((nb,)),
        dma((nb,)),
        dma((ng,)),
        dma((ng,)),
        dma((ng, nb)),
        dma((ng, nb)),
        dma(()),
        dma(()),
        dma((ng,)),
        dma((ng,)),
        dma((nb,)),
        dma((nb,)),
        dma((nd,)),
        dma((nd,)),
    ]
    potentials, mass = pl.pallas_call(
        functools.partial(kernel, ng, nb, cap, out_rows),
        out_shape=shapes,
        in_specs=[hbm, hbm, hbm, hbm, smem, hbm, hbm, hbm, hbm, hbm, smem, hbm],
        out_specs=(hbm, vmem),
        scratch_shapes=scratch,
        compiler_params=pltpu.CompilerParams(
            collective_id=0, has_side_effects=True, vmem_limit_bytes=56 * 1024 * 1024
        ),
    )(
        node_modes,
        node_index,
        interp,
        normals,
        counts.reshape(1, nd),
        inverse_diag,
        *factors,
        ranks,
        areas,
    )
    return pl.pallas_call(
        hand_over,
        out_shape=shapes,
        in_specs=[hbm, vmem],
        out_specs=(vmem, vmem),
        scratch_shapes=[dma(())],
        compiler_params=pltpu.CompilerParams(vmem_limit_bytes=56 * 1024 * 1024),
    )(potentials, mass)


def solution(mesh):
    split_rows = P(("grp", "blk"), None)
    split_cols = P(None, ("grp", "blk"))
    in_specs = (
        P(None, ("grp", "blk"), "side"),
        split_cols,
        split_cols,
        split_cols,
        split_cols,
        split_rows,
        split_rows,
        split_rows,
        split_rows,
        split_rows,
        P(("grp", "blk")),
        P(("grp", "blk")),
    )
    out_specs = (P(("grp", "blk"), "side"), P(("grp", "blk"), "side"))
    return jax.shard_map(body, mesh=mesh, in_specs=in_specs, out_specs=out_specs, check_vma=False)
```

```python
import functools

import jax
import jax.numpy as jnp
from jax import lax
from jax.experimental import pallas as pl
from jax.experimental.pallas import tpu as pltpu
from jax.sharding import PartitionSpec as P

MESH = pl.DeviceIdType.MESH
F32 = jnp.float32
BF16 = jnp.bfloat16
TILE = 16
LANES = 128
NODE_TILE = 256


def dot(a, b):
    return jnp.dot(a, b, preferred_element_type=F32)


def dot_rows(a, b):
    return lax.dot_general(a, b, (((0,), (0,)), ((), ())), preferred_element_type=F32)


def dot_lanes(a, b):
    return lax.dot_general(a, b, (((1,), (1,)), ((), ())), preferred_element_type=F32)


def split(a):
    high = a.astype(BF16)
    return high, (a - high.astype(F32)).astype(BF16)


def kernel(
    ng,
    nb,
    cap,
    out_rows,
    modes_hbm,
    index_hbm,
    interp_hbm,
    normals_hbm,
    counts,
    diag_hbm,
    ll_hbm,
    lr_hbm,
    ul_hbm,
    ur_hbm,
    ranks,
    areas_hbm,
    pot,
    mass_ref,
    modes,
    index,
    interp,
    normals,
    diag,
    ll,
    lr,
    ul,
    ur,
    areas,
    rows_pack,
    modes_t,
    wbuf,
    sendbuf,
    arrived,
    pick,
    maps,
    left,
    record,
    back_terms,
    kout,
    wcat,
    gp,
    bu,
    solved,
    velocities,
    velocities_t,
    zall,
    psend,
    precv,
    msend,
    mrecv,
    local_sem,
    map_send,
    map_recv,
    slab_send,
    slab_recv,
    vel_send,
    vel_recv,
    side_send,
    side_recv,
    z_send,
    z_recv,
    p_send,
    p_recv,
    m_send,
    m_recv,
):
    nd = ng * nb
    rank_width = ll.shape[0]
    two = 2 * rank_width
    panels = diag.shape[0]
    nodes, width = modes.shape[1:]
    slots = nd * cap
    side, my_g, my_b = lax.axis_index("side"), lax.axis_index("grp"), lax.axis_index("blk")
    me = my_g * nb + my_b

    barrier = pltpu.get_barrier_semaphore()

    @pl.loop(1, nd)
    def _(k):
        other = lax.rem(me + k, nd)
        pl.semaphore_signal(
            barrier, inc=1, device_id=(side, other // nb, lax.rem(other, nb)), device_id_type=MESH
        )

    pl.semaphore_signal(barrier, inc=1, device_id=(1 - side, my_g, my_b), device_id_type=MESH)

    pairs = [
        (diag_hbm, diag),
        (lr_hbm, lr),
        (ur_hbm, ur),
        (ll_hbm, ll),
        (ul_hbm, ul),
        (index_hbm, index),
        (interp_hbm, interp),
        (normals_hbm, normals),
        (areas_hbm, areas),
    ] + [(modes_hbm.at[c], modes.at[c]) for c in range(3)]
    loads = [pltpu.make_async_copy(a, b, local_sem.at[i]) for i, (a, b) in enumerate(pairs)]
    for load in (*loads[5:8], *loads[9:12], *loads[0:5], loads[8]):
        load.start()

    for i in (5, 6, 7):
        loads[i].wait()
    tile_of = index[...] // NODE_TILE
    rows_pack[0:4, :] = (index[...] - tile_of * NODE_TILE).astype(F32)
    for tile in range(nodes // NODE_TILE):
        rows_pack[4 * tile + 4 : 4 * tile + 8, :] = jnp.where(tile_of == tile, interp[...], 0.0)

    def map_copy(k, b):
        return pltpu.make_async_remote_copy(
            src_ref=maps.at[me],
            dst_ref=maps.at[me],
            send_sem=map_send.at[k],
            recv_sem=map_recv.at[k],
            device_id=(side, my_g, b),
            device_id_type=MESH,
        )

    def slab_copy(k, g):
        return pltpu.make_async_remote_copy(
            src_ref=maps.at[pl.ds(my_g * nb, nb)],
            dst_ref=maps.at[pl.ds(my_g * nb, nb)],
            send_sem=slab_send.at[k],
            recv_sem=slab_recv.at[k],
            device_id=(side, g, my_b),
            device_id_type=MESH,
        )

    def vel_copy(kg, kb, g, b):
        return pltpu.make_async_remote_copy(
            src_ref=sendbuf.at[g * nb + b],
            dst_ref=arrived.at[me],
            send_sem=vel_send.at[kg, kb],
            recv_sem=vel_recv.at[kg, kb],
            device_id=(side, g, b),
            device_id_type=MESH,
        )

    chunk = nb * cap
    node_ids = [
        (lax.broadcasted_iota(jnp.int32, (TILE, LANES), 0) + part * TILE).astype(F32).astype(BF16)
        for part in range(NODE_TILE // TILE)
    ]
    zero16 = jnp.zeros((TILE, LANES), BF16)

    def weights(g):
        @pl.loop(0, chunk // LANES)
        def _(q):
            here = pl.ds(pl.multiple_of(g * chunk + q * LANES, LANES), LANES)
            there = pl.ds(pl.multiple_of(q * LANES, LANES), LANES)

            def wide(r):
                row = rows_pack[r : r + 1, here]
                return jnp.broadcast_to(row, (TILE, LANES)).astype(BF16)

            places = [wide(k) for k in range(4)]
            for tile in range(nodes // NODE_TILE):
                worth = [wide(4 * tile + 4 + k) for k in range(4)]
                for part, ids in enumerate(node_ids):
                    terms = [jnp.where(ids == places[k], worth[k], zero16) for k in range(4)]
                    start = tile * NODE_TILE + part * TILE
                    wbuf[start : start + TILE, there] = (terms[0] + terms[1]) + (terms[2] + terms[3])

    def velocity_chunk(g):
        weights(g)
        moved = dot(modes_t[...], wbuf[...])
        normal = normals[:, pl.ds(pl.multiple_of(g * chunk, LANES), chunk)]
        velocity = normal[0:1] * moved[0:width]
        for c in (1, 2):
            velocity += normal[c : c + 1] * moved[c * width : (c + 1) * width]
        sendbuf[pl.ds(g * nb, nb)] = velocity.T.astype(BF16).reshape(nb, cap, width)

    def velocity_send(kg, g):
        @pl.loop(1, jnp.where(kg == 0, nb, nb + 1))
        def _(k):
            vel_copy(kg, lax.rem(k, nb), g, lax.rem(my_b + k, nb)).start()

    first = lax.rem(my_g + 1, ng)
    for i in (9, 10, 11):
        loads[i].wait()
    for c in range(3):
        modes_t[c * width : (c + 1) * width, :] = modes[c].T
    velocity_chunk(first)
    pl.semaphore_wait(barrier, nd)
    velocity_send(lax.rem(jnp.int32(1), ng), first)

    for i in range(5):
        loads[i].wait()
    keep = lax.broadcasted_iota(jnp.int32, (rank_width, panels), 0) < ranks[0]
    lower = jnp.where(keep, ll[...].astype(F32), 0.0).astype(BF16)
    upper = jnp.where(keep, ul[...].astype(F32), 0.0).astype(BF16)
    right = jnp.concatenate([lr[...], ur[...]], axis=0)
    w_high, w_low = split(dot(right, diag[...]))
    wcat[0:two, :] = w_high
    wcat[two : 2 * two, :] = w_low
    both = dot_lanes(wcat[...], lower)
    both = both[0:two] + both[two : 2 * two]
    top = dot_lanes(ur[...], upper)
    maps[me] = jnp.concatenate(
        [both[0:rank_width], both[rank_width:two], top, jnp.zeros_like(top)], axis=1
    )

    @pl.loop(1, nb)
    def _(k):
        map_copy(k, lax.rem(my_b + k, nb)).start()

    lower_t = lower.astype(F32).T.astype(BF16)
    upper_t = upper.astype(F32).T.astype(BF16)
    bu[:, width : width + rank_width] = lower_t
    gp[:, 3 * rank_width : 4 * rank_width] = upper_t
    gp[:, 4 * rank_width : 5 * rank_width] = upper_t

    def rest(step):
        kg = lax.rem(step + 1, ng)
        g = lax.rem(my_g + kg, ng)
        velocity_chunk(g)
        velocity_send(kg, g)

    rest(jnp.int32(1))

    @pl.loop(1, nb)
    def _(k):
        map_copy(k, lax.rem(my_b + k, nb)).wait()

    @pl.loop(1, ng)
    def _(k):
        slab_copy(k, lax.rem(my_g + k, ng)).start()

    pl.loop(2, ng)(rest)

    arrived[me] = sendbuf[me]

    slot_ids = lax.broadcasted_iota(jnp.int32, (1, slots), 1)

    def place(j, carry):
        offset, target = carry
        local = slot_ids - j * cap
        count = counts[0, j]
        target = jnp.where((local >= 0) & (local < count), local + offset, target)
        return offset + count, target

    _, target = lax.fori_loop(
        0, nd, place, (jnp.int32(0), jnp.full((1, slots), -1, jnp.int32))
    )
    panel_ids = lax.broadcasted_iota(jnp.int32, (TILE, slots), 0)

    per_step = panels // TILE // (2 * nb)

    def pick_rows(step):
        for r in range(per_step):
            i = step * per_step + r
            hot = jnp.where(panel_ids + i * TILE == target, 1.0, 0.0)
            pick[pl.ds(pl.multiple_of(i * TILE, TILE), TILE), :] = hot.astype(BF16)

    @pl.loop(1, ng)
    def _(k):
        slab_copy(k, lax.rem(my_g + k, ng)).wait()

    units = ng * two
    span = 4 * rank_width

    def three(high, low):
        return jnp.concatenate([high, low, high], axis=1)

    def state(s):
        high, low = split(s)
        return jnp.concatenate([high, high, low], axis=0)

    @pl.loop(0, nd, unroll=4)
    def _(i):
        high, low = split(maps[i])
        for c in range(3):
            part = slice(c * rank_width, (c + 1) * rank_width)
            left[i, part, :] = three(high[:, part], low[:, part])

    row_id = lax.broadcasted_iota(jnp.int32, (rank_width, span), 0)
    col_id = lax.broadcasted_iota(jnp.int32, (rank_width, span), 1)

    def unit(place):
        return jnp.where(col_id == row_id + place * rank_width, 1.0, 0.0)

    def forward(b, states):
        hit = jnp.where(b == my_b, 1.0, 0.0)
        after = []
        for g in range(ng):
            i = g * nb + b
            record[i, 0:rank_width, :] = states[g]
            moved = dot(left[i, 0:two, :], state(states[g]))
            back_terms[i] = moved[rank_width:two]
            after.append(states[g] - moved[0:rank_width] + hit * unit(2))
        pick_rows(b)
        return tuple(after)

    def backward(step, states):
        b = nb - 1 - step
        hit = jnp.where(b == my_b, 1.0, 0.0)
        after = []
        for g in range(ng):
            i = g * nb + b
            record[i, rank_width:two, :] = states[g]
            moved = dot(left[i, two : 3 * rank_width, :], state(states[g]))
            after.append(states[g] + (hit * unit(3) - back_terms[i]) - moved)
        pick_rows(nb + step)
        return tuple(after)

    ahead = lax.fori_loop(0, nb, forward, (unit(1),) * ng)
    behind = lax.fori_loop(0, nb, backward, (unit(0),) * ng)

    row_two = lax.broadcasted_iota(jnp.int32, (two, units), 0)
    col_two = lax.broadcasted_iota(jnp.int32, (two, units), 1)

    def terms_of(g):
        return jnp.where(col_two == row_two + two * g, 1.0, 0.0).astype(BF16)

    nothing = jnp.zeros((rank_width, units), F32)

    def across(lhs, t, s, g):
        l_high, l_low = split(lhs)
        t_high, t_low = split(t)
        s_high, s_low = split(s)
        own = terms_of(g)
        high = jnp.concatenate([t_high, s_high, own], axis=0)
        low = jnp.concatenate([t_low, s_low, jnp.zeros_like(own)], axis=0)
        return dot(l_high, high) + dot(l_low, high) + dot(l_high, low)

    s_in, t_in = [nothing], [nothing]
    for g in range(ng - 1):
        s_in.append(across(ahead[g], nothing, s_in[g], g))
    for g in range(ng - 1, 0, -1):
        t_in.append(across(behind[g], t_in[-1], s_in[g], g))
    t_in = t_in[::-1]
    s_here, t_here = nothing, nothing
    for g in range(ng):
        s_here = jnp.where(my_g == g, s_in[g], s_here)
        t_here = jnp.where(my_g == g, t_in[g], t_here)
    mine = record[pl.ds(my_g * nb, nb)].reshape(nb * two, span)
    k_high, k_low = split(across(mine, t_here, s_here, my_g))
    kout[:, 0:units] = k_high
    kout[:, units : 2 * units] = k_low

    loads[8].wait()
    area = areas[...].T

    @pl.loop(0, nd - 1)
    def _(k):
        source = k + 1
        vel_copy(source // nb, lax.rem(source, nb), my_g, my_b).wait_recv()

    b = dot(pick[...], arrived[...].reshape(slots, width)).astype(BF16)
    velocities[side] = b
    side_copy = pltpu.make_async_remote_copy(
        src_ref=velocities.at[side],
        dst_ref=velocities.at[side],
        send_sem=side_send,
        recv_sem=side_recv,
        device_id=(1 - side, my_g, my_b),
        device_id_type=MESH,
    )
    z = dot(wcat[...], b)
    zall[my_g] = (z[0:two] + z[two : 2 * two]).astype(BF16)

    def z_copy(k, g):
        return pltpu.make_async_remote_copy(
            src_ref=zall.at[my_g],
            dst_ref=zall.at[my_g],
            send_sem=z_send.at[k],
            recv_sem=z_recv.at[k],
            device_id=(side, g, my_b),
            device_id_type=MESH,
        )

    @pl.loop(1, ng)
    def _(k):
        z_copy(k, lax.rem(my_g + k, ng)).start()

    side_copy.start()
    bu[:, 0:width] = b
    both = dot(diag[...], bu[...])
    solved[...] = both[:, 0:width]
    g_high, g_low = split(both[:, width : width + rank_width])
    gp[:, 0:rank_width] = g_high
    gp[:, rank_width:two] = g_low
    gp[:, two : 3 * rank_width] = g_high

    @pl.loop(1, ng)
    def _(k):
        z_copy(k, lax.rem(my_g + k, ng)).wait()

    zcat = zall[...].reshape(units, width)
    part = dot(kout[...], jnp.concatenate([zcat, zcat], axis=0))
    psend[...] = part.astype(BF16).reshape(nb, two, width)

    def p_copy(k, b):
        return pltpu.make_async_remote_copy(
            src_ref=psend.at[b],
            dst_ref=precv.at[my_b],
            send_sem=p_send.at[k],
            recv_sem=p_recv.at[k],
            device_id=(side, my_g, b),
            device_id_type=MESH,
        )

    @pl.loop(1, nb)
    def _(k):
        p_copy(k, lax.rem(my_b + k, nb)).start()

    precv[my_b] = psend[my_b]
    side_copy.wait()
    for h in range(2):
        velocities_t[h * width : (h + 1) * width, :] = velocities[h].T

    @pl.loop(1, nb)
    def _(k):
        p_copy(k, lax.rem(my_b + k, nb)).wait()

    states = jnp.sum(precv[...].astype(F32), axis=0)
    s_high, s_low = split(states[0:rank_width])
    t_high, t_low = split(states[rank_width:two])
    rhs = jnp.concatenate([s_high, s_high, s_low, t_high, t_low], axis=0)
    potentials = (solved[...] - dot(gp[...], rhs)).astype(BF16)
    pot[...] = potentials
    weighted = (area[:, 0:1] * potentials.astype(F32)).astype(BF16)
    partial = dot(velocities_t[...], weighted).astype(BF16)
    held = msend.shape[1]
    if held != out_rows:
        row = lax.broadcasted_iota(jnp.int32, (nd * held, nd * out_rows), 0)
        col = lax.broadcasted_iota(jnp.int32, (nd * held, nd * out_rows), 1)
        home = (col // out_rows) * held + col % out_rows
        partial = dot(jnp.where(row == home, 1.0, 0.0).astype(BF16), partial).astype(BF16)
    msend[...] = partial.reshape(nd, held, width)

    def m_copy(k, d):
        return pltpu.make_async_remote_copy(
            src_ref=msend.at[d],
            dst_ref=mrecv.at[me],
            send_sem=m_send.at[k],
            recv_sem=m_recv.at[k],
            device_id=(side, d // nb, lax.rem(d, nb)),
            device_id_type=MESH,
        )

    @pl.loop(1, nd)
    def _(k):
        m_copy(k, lax.rem(me + k, nd)).start()

    mrecv[me] = msend[me]

    @pl.loop(0, nd - 1)
    def _(k):
        source = k + 1
        vel_copy(source // nb, lax.rem(source, nb), my_g, my_b).wait_send()

    @pl.loop(1, nd)
    def _(k):
        m_copy(k, lax.rem(me + k, nd)).wait()

    mass_ref[...] = jnp.sum(mrecv[...].astype(F32), axis=0)[0:out_rows]


def hand_over(pot_in, mass_in, pot_out, mass_out, sems):
    copies = (
        pltpu.make_async_copy(pot_in, pot_out, sems.at[0]),
        pltpu.make_async_copy(mass_in, mass_out, sems.at[1]),
    )
    for copy in copies:
        copy.start()
    for copy in copies:
        copy.wait()


def body(
    node_modes,
    node_index,
    interp,
    normals,
    counts,
    inverse_diag,
    lower_left,
    lower_right,
    upper_left,
    upper_right,
    ranks,
    areas,
):
    ng, nb = lax.axis_size("grp"), lax.axis_size("blk")
    nd = ng * nb
    nodes, width = node_modes.shape[1:]
    cap_given = node_index.shape[1] // nd
    cap = -(-cap_given // TILE) * TILE
    if cap != cap_given:

        def widen(part):
            lead = part.shape[0]
            spare = ((0, 0), (0, 0), (0, cap - cap_given))
            return jnp.pad(part.reshape(lead, nd, cap_given), spare).reshape(lead, nd * cap)

        node_index, interp, normals = widen(node_index), widen(interp), widen(normals)
    slots = nd * cap
    panels = inverse_diag.shape[0]
    rank_width = lower_left.shape[1]
    factors = [part.T for part in (lower_left, lower_right, upper_left, upper_right)]
    two = 2 * rank_width
    units = ng * two
    out_rows = 2 * width // nd
    held = -(-out_rows // TILE) * TILE
    areas = areas.reshape(1, panels)
    shapes = (
        jax.ShapeDtypeStruct((panels, width), BF16),
        jax.ShapeDtypeStruct((out_rows, width), F32),
    )
    hbm = pl.BlockSpec(memory_space=pltpu.HBM)
    smem = pl.BlockSpec(memory_space=pltpu.SMEM)
    vmem = pl.BlockSpec(memory_space=pltpu.VMEM)
    dma = pltpu.SemaphoreType.DMA
    factor = pltpu.VMEM((rank_width, panels), BF16)
    scratch = [
        pltpu.VMEM((3, nodes, width), BF16),
        pltpu.VMEM((4, slots), jnp.int32),
        pltpu.VMEM((4, slots), F32),
        pltpu.VMEM((3, slots), F32),
        pltpu.VMEM((panels, panels), BF16),
        factor,
        factor,
        factor,
        factor,
        pltpu.VMEM((1, panels), F32),
        pltpu.VMEM((4 + 4 * (nodes // NODE_TILE), slots), F32),
        pltpu.VMEM((3 * width, nodes), BF16),
        pltpu.VMEM((nodes, nb * cap), BF16),
        pltpu.VMEM((nd, cap, width), BF16),
        pltpu.VMEM((nd, cap, width), BF16),
        pltpu.VMEM((panels, slots), BF16),
        pltpu.VMEM((nd, rank_width, 4 * rank_width), F32),
        pltpu.VMEM((nd, 3 * rank_width, 3 * rank_width), BF16),
        pltpu.VMEM((nd, two, 4 * rank_width), F32),
        pltpu.VMEM((nd, rank_width, 4 * rank_width), F32),
        pltpu.VMEM((nb * two, 2 * units), BF16),
        pltpu.VMEM((2 * two, panels), BF16),
        pltpu.VMEM((panels, 5 * rank_width), BF16),
        pltpu.VMEM((panels, width + rank_width), BF16),
        pltpu.VMEM((panels, width), F32),
        pltpu.VMEM((2, panels, width), BF16),
        pltpu.VMEM((2 * width, panels), BF16),
        pltpu.VMEM((ng, two, width), BF16),
        pltpu.VMEM((nb, two, width), BF16),
        pltpu.VMEM((nb, two, width), BF16),
        pltpu.VMEM((nd, held, width), BF16),
        pltpu.VMEM((nd, held, width), BF16),
        dma((12,)),
        dma((nb,)),
        dma((nb,)),
        dma((ng,)),
        dma((ng,)),
        dma((ng, nb)),
        dma((ng, nb)),
        dma(()),
        dma(()),
        dma((ng,)),
        dma((ng,)),
        dma((nb,)),
        dma((nb,)),
        dma((nd,)),
        dma((nd,)),
    ]
    potentials, mass = pl.pallas_call(
        functools.partial(kernel, ng, nb, cap, out_rows),
        out_shape=(pltpu.VMEM((panels, width), BF16), pltpu.VMEM((out_rows, width), F32)),
        in_specs=[hbm, hbm, hbm, hbm, smem, hbm, hbm, hbm, hbm, hbm, smem, hbm],
        out_specs=(vmem, vmem),
        scratch_shapes=scratch,
        compiler_params=pltpu.CompilerParams(
            collective_id=0, has_side_effects=True, vmem_limit_bytes=56 * 1024 * 1024
        ),
    )(
        node_modes,
        node_index,
        interp,
        normals,
        counts.reshape(1, nd),
        inverse_diag,
        *factors,
        ranks,
        areas,
    )
    return pl.pallas_call(
        hand_over,
        out_shape=shapes,
        in_specs=[vmem, vmem],
        out_specs=(hbm, hbm),
        scratch_shapes=[dma((2,))],
    )(potentials, mass)


def solution(mesh):
    split_rows = P(("grp", "blk"), None)
    split_cols = P(None, ("grp", "blk"))
    in_specs = (
        P(None, ("grp", "blk"), "side"),
        split_cols,
        split_cols,
        split_cols,
        split_cols,
        split_rows,
        split_rows,
        split_rows,
        split_rows,
        split_rows,
        P(("grp", "blk")),
        P(("grp", "blk")),
    )
    out_specs = (P(("grp", "blk"), "side"), P(("grp", "blk"), "side"))
    return jax.shard_map(body, mesh=mesh, in_specs=in_specs, out_specs=out_specs, check_vma=False)
```

```python
import functools

import jax
import jax.numpy as jnp
from jax import lax
from jax.experimental import pallas as pl
from jax.experimental.pallas import tpu as pltpu
from jax.sharding import PartitionSpec as P

MESH = pl.DeviceIdType.MESH
F32 = jnp.float32
BF16 = jnp.bfloat16
TILE = 16
LANES = 128
NODE_TILE = 256


def dot(a, b):
    return jnp.dot(a, b, preferred_element_type=F32)


def dot_rows(a, b):
    return lax.dot_general(a, b, (((0,), (0,)), ((), ())), preferred_element_type=F32)


def dot_lanes(a, b):
    return lax.dot_general(a, b, (((1,), (1,)), ((), ())), preferred_element_type=F32)


def split(a):
    high = a.astype(BF16)
    return high, (a - high.astype(F32)).astype(BF16)


def kernel(
    ng,
    nb,
    cap,
    out_rows,
    modes_hbm,
    index_hbm,
    interp_hbm,
    normals_hbm,
    counts,
    diag_hbm,
    ll_hbm,
    lr_hbm,
    ul_hbm,
    ur_hbm,
    ranks,
    areas_hbm,
    pot,
    mass_ref,
    modes,
    index,
    interp,
    normals,
    diag,
    ll,
    lr,
    ul,
    ur,
    areas,
    rows_pack,
    modes_t,
    wbuf,
    sendbuf,
    arrived,
    pick,
    maps,
    left,
    record,
    back_terms,
    kout,
    wcat,
    gp,
    bu,
    solved,
    velocities,
    velocities_t,
    zall,
    psend,
    precv,
    msend,
    mrecv,
    local_sem,
    map_send,
    map_recv,
    slab_send,
    slab_recv,
    vel_send,
    vel_recv,
    side_send,
    side_recv,
    k_send,
    k_recv,
    ready,
    z_send,
    z_recv,
    p_send,
    p_recv,
    m_send,
    m_recv,
):
    nd = ng * nb
    rank_width = ll.shape[0]
    two = 2 * rank_width
    panels = diag.shape[0]
    nodes, width = modes.shape[1:]
    slots = nd * cap
    side, my_g, my_b = lax.axis_index("side"), lax.axis_index("grp"), lax.axis_index("blk")
    me = my_g * nb + my_b

    barrier = pltpu.get_barrier_semaphore()

    @pl.loop(1, nd)
    def _(k):
        other = lax.rem(me + k, nd)
        pl.semaphore_signal(
            barrier, inc=1, device_id=(side, other // nb, lax.rem(other, nb)), device_id_type=MESH
        )

    other_side = (1 - side, my_g, my_b)

    @pl.when(side == 0)
    def _():
        pl.semaphore_signal(barrier, inc=1, device_id=other_side, device_id_type=MESH)

    pairs = [
        (diag_hbm, diag),
        (lr_hbm, lr),
        (ur_hbm, ur),
        (ll_hbm, ll),
        (ul_hbm, ul),
        (index_hbm, index),
        (interp_hbm, interp),
        (normals_hbm, normals),
        (areas_hbm, areas),
    ] + [(modes_hbm.at[c], modes.at[c]) for c in range(3)]
    loads = [pltpu.make_async_copy(a, b, local_sem.at[i]) for i, (a, b) in enumerate(pairs)]
    for load in (*loads[5:8], *loads[9:12], *loads[0:5], loads[8]):
        load.start()

    for i in (5, 6, 7):
        loads[i].wait()
    tile_of = index[...] // NODE_TILE
    rows_pack[0:4, :] = (index[...] - tile_of * NODE_TILE).astype(F32)
    for tile in range(nodes // NODE_TILE):
        rows_pack[4 * tile + 4 : 4 * tile + 8, :] = jnp.where(tile_of == tile, interp[...], 0.0)

    def map_copy(k, b):
        return pltpu.make_async_remote_copy(
            src_ref=maps.at[me],
            dst_ref=maps.at[me],
            send_sem=map_send.at[k],
            recv_sem=map_recv.at[k],
            device_id=(side, my_g, b),
            device_id_type=MESH,
        )

    def slab_copy(k, g):
        return pltpu.make_async_remote_copy(
            src_ref=maps.at[pl.ds(my_g * nb, nb)],
            dst_ref=maps.at[pl.ds(my_g * nb, nb)],
            send_sem=slab_send.at[k],
            recv_sem=slab_recv.at[k],
            device_id=(side, g, my_b),
            device_id_type=MESH,
        )

    def vel_copy(kg, kb, g, b):
        return pltpu.make_async_remote_copy(
            src_ref=sendbuf.at[g * nb + b],
            dst_ref=arrived.at[me],
            send_sem=vel_send.at[kg, kb],
            recv_sem=vel_recv.at[kg, kb],
            device_id=(side, g, b),
            device_id_type=MESH,
        )

    chunk = nb * cap
    node_ids = [
        (lax.broadcasted_iota(jnp.int32, (TILE, LANES), 0) + part * TILE).astype(F32).astype(BF16)
        for part in range(NODE_TILE // TILE)
    ]
    zero16 = jnp.zeros((TILE, LANES), BF16)

    def weights(g):
        @pl.loop(0, chunk // LANES)
        def _(q):
            here = pl.ds(pl.multiple_of(g * chunk + q * LANES, LANES), LANES)
            there = pl.ds(pl.multiple_of(q * LANES, LANES), LANES)

            def wide(r):
                row = rows_pack[r : r + 1, here]
                return jnp.broadcast_to(row, (TILE, LANES)).astype(BF16)

            places = [wide(k) for k in range(4)]
            for tile in range(nodes // NODE_TILE):
                worth = [wide(4 * tile + 4 + k) for k in range(4)]
                for part, ids in enumerate(node_ids):
                    terms = [jnp.where(ids == places[k], worth[k], zero16) for k in range(4)]
                    start = tile * NODE_TILE + part * TILE
                    wbuf[start : start + TILE, there] = (terms[0] + terms[1]) + (terms[2] + terms[3])

    def velocity_chunk(g):
        weights(g)
        moved = dot(modes_t[...], wbuf[...])
        normal = normals[:, pl.ds(pl.multiple_of(g * chunk, LANES), chunk)]
        velocity = normal[0:1] * moved[0:width]
        for c in (1, 2):
            velocity += normal[c : c + 1] * moved[c * width : (c + 1) * width]
        sendbuf[pl.ds(g * nb, nb)] = velocity.T.astype(BF16).reshape(nb, cap, width)

    def velocity_send(kg, g):
        @pl.loop(1, jnp.where(kg == 0, nb, nb + 1))
        def _(k):
            vel_copy(kg, lax.rem(k, nb), g, lax.rem(my_b + k, nb)).start()

    first = lax.rem(my_g + 1, ng)
    for i in (9, 10, 11):
        loads[i].wait()
    for c in range(3):
        modes_t[c * width : (c + 1) * width, :] = modes[c].T
    velocity_chunk(first)
    pl.semaphore_wait(barrier, nd - 1 + side)

    @pl.when(side == 1)
    def _():
        pl.semaphore_signal(ready, inc=1, device_id=other_side, device_id_type=MESH)

    velocity_send(lax.rem(jnp.int32(1), ng), first)

    for i in range(5):
        loads[i].wait()
    keep = lax.broadcasted_iota(jnp.int32, (rank_width, panels), 0) < ranks[0]
    lower = jnp.where(keep, ll[...].astype(F32), 0.0).astype(BF16)
    upper = jnp.where(keep, ul[...].astype(F32), 0.0).astype(BF16)
    right = jnp.concatenate([lr[...], ur[...]], axis=0)
    w_high, w_low = split(dot(right, diag[...]))
    wcat[0:two, :] = w_high
    wcat[two : 2 * two, :] = w_low
    @pl.when(side == 0)
    def _():
        both = dot_lanes(wcat[...], lower)
        both = both[0:two] + both[two : 2 * two]
        top = dot_lanes(ur[...], upper)
        maps[me] = jnp.concatenate(
            [both[0:rank_width], both[rank_width:two], top, jnp.zeros_like(top)], axis=1
        )

        @pl.loop(1, nb)
        def _(k):
            map_copy(k, lax.rem(my_b + k, nb)).start()

    lower_t = lower.astype(F32).T.astype(BF16)
    upper_t = upper.astype(F32).T.astype(BF16)
    bu[:, width : width + rank_width] = lower_t
    gp[:, 3 * rank_width : 4 * rank_width] = upper_t
    gp[:, 4 * rank_width : 5 * rank_width] = upper_t

    def rest(step):
        kg = lax.rem(step + 1, ng)
        g = lax.rem(my_g + kg, ng)
        velocity_chunk(g)
        velocity_send(kg, g)

    rest(jnp.int32(1))

    @pl.when(side == 0)
    def _():
        @pl.loop(1, nb)
        def _(k):
            map_copy(k, lax.rem(my_b + k, nb)).wait()

        @pl.loop(1, ng)
        def _(k):
            slab_copy(k, lax.rem(my_g + k, ng)).start()

    pl.loop(2, ng)(rest)

    arrived[me] = sendbuf[me]

    slot_ids = lax.broadcasted_iota(jnp.int32, (1, slots), 1)

    def place(j, carry):
        offset, target = carry
        local = slot_ids - j * cap
        count = counts[0, j]
        target = jnp.where((local >= 0) & (local < count), local + offset, target)
        return offset + count, target

    _, target = lax.fori_loop(
        0, nd, place, (jnp.int32(0), jnp.full((1, slots), -1, jnp.int32))
    )
    panel_ids = lax.broadcasted_iota(jnp.int32, (TILE, slots), 0)

    per_step = panels // TILE // (2 * nb)

    def pick_rows(step):
        for r in range(per_step):
            i = step * per_step + r
            hot = jnp.where(panel_ids + i * TILE == target, 1.0, 0.0)
            pick[pl.ds(pl.multiple_of(i * TILE, TILE), TILE), :] = hot.astype(BF16)

    @pl.when(side == 1)
    def _():
        pl.loop(0, 2 * nb)(pick_rows)

    kout_copy = pltpu.make_async_remote_copy(
        src_ref=kout,
        dst_ref=kout,
        send_sem=k_send,
        recv_sem=k_recv,
        device_id=other_side,
        device_id_type=MESH,
    )
    units = ng * two
    span = 4 * rank_width

    @pl.when(side == 0)
    def _():
        @pl.loop(1, ng)
        def _(k):
            slab_copy(k, lax.rem(my_g + k, ng)).wait()

        def three(high, low):
            return jnp.concatenate([high, low, high], axis=1)

        def state(s):
            high, low = split(s)
            return jnp.concatenate([high, high, low], axis=0)

        @pl.loop(0, nd, unroll=4)
        def _(i):
            high, low = split(maps[i])
            for c in range(3):
                part = slice(c * rank_width, (c + 1) * rank_width)
                left[i, part, :] = three(high[:, part], low[:, part])

        row_id = lax.broadcasted_iota(jnp.int32, (rank_width, span), 0)
        col_id = lax.broadcasted_iota(jnp.int32, (rank_width, span), 1)

        def unit(place):
            return jnp.where(col_id == row_id + place * rank_width, 1.0, 0.0)

        def forward(b, states):
            hit = jnp.where(b == my_b, 1.0, 0.0)
            after = []
            for g in range(ng):
                i = g * nb + b
                record[i, 0:rank_width, :] = states[g]
                moved = dot(left[i, 0:two, :], state(states[g]))
                back_terms[i] = moved[rank_width:two]
                after.append(states[g] - moved[0:rank_width] + hit * unit(2))
            pick_rows(b)
            return tuple(after)

        def backward(step, states):
            b = nb - 1 - step
            hit = jnp.where(b == my_b, 1.0, 0.0)
            after = []
            for g in range(ng):
                i = g * nb + b
                record[i, rank_width:two, :] = states[g]
                moved = dot(left[i, two : 3 * rank_width, :], state(states[g]))
                after.append(states[g] + (hit * unit(3) - back_terms[i]) - moved)
            pick_rows(nb + step)
            return tuple(after)

        ahead = lax.fori_loop(0, nb, forward, (unit(1),) * ng)
        behind = lax.fori_loop(0, nb, backward, (unit(0),) * ng)

        row_two = lax.broadcasted_iota(jnp.int32, (two, units), 0)
        col_two = lax.broadcasted_iota(jnp.int32, (two, units), 1)

        def terms_of(g):
            return jnp.where(col_two == row_two + two * g, 1.0, 0.0).astype(BF16)

        nothing = jnp.zeros((rank_width, units), F32)

        def across(lhs, t, s, g):
            l_high, l_low = split(lhs)
            t_high, t_low = split(t)
            s_high, s_low = split(s)
            own = terms_of(g)
            high = jnp.concatenate([t_high, s_high, own], axis=0)
            low = jnp.concatenate([t_low, s_low, jnp.zeros_like(own)], axis=0)
            return dot(l_high, high) + dot(l_low, high) + dot(l_high, low)

        s_in, t_in = [nothing], [nothing]
        for g in range(ng - 1):
            s_in.append(across(ahead[g], nothing, s_in[g], g))
        for g in range(ng - 1, 0, -1):
            t_in.append(across(behind[g], t_in[-1], s_in[g], g))
        t_in = t_in[::-1]
        s_here, t_here = nothing, nothing
        for g in range(ng):
            s_here = jnp.where(my_g == g, s_in[g], s_here)
            t_here = jnp.where(my_g == g, t_in[g], t_here)
        mine = record[pl.ds(my_g * nb, nb)].reshape(nb * two, span)
        k_high, k_low = split(across(mine, t_here, s_here, my_g))
        kout[:, 0:units] = k_high
        kout[:, units : 2 * units] = k_low
        pl.semaphore_wait(ready, 1)
        kout_copy.start()

    loads[8].wait()
    area = areas[...].T

    @pl.loop(0, nd - 1)
    def _(k):
        source = k + 1
        vel_copy(source // nb, lax.rem(source, nb), my_g, my_b).wait_recv()

    b = dot(pick[...], arrived[...].reshape(slots, width)).astype(BF16)
    velocities[side] = b
    side_copy = pltpu.make_async_remote_copy(
        src_ref=velocities.at[side],
        dst_ref=velocities.at[side],
        send_sem=side_send,
        recv_sem=side_recv,
        device_id=(1 - side, my_g, my_b),
        device_id_type=MESH,
    )
    z = dot(wcat[...], b)
    zall[my_g] = (z[0:two] + z[two : 2 * two]).astype(BF16)

    def z_copy(k, g):
        return pltpu.make_async_remote_copy(
            src_ref=zall.at[my_g],
            dst_ref=zall.at[my_g],
            send_sem=z_send.at[k],
            recv_sem=z_recv.at[k],
            device_id=(side, g, my_b),
            device_id_type=MESH,
        )

    @pl.loop(1, ng)
    def _(k):
        z_copy(k, lax.rem(my_g + k, ng)).start()

    side_copy.start()
    bu[:, 0:width] = b
    both = dot(diag[...], bu[...])
    solved[...] = both[:, 0:width]
    g_high, g_low = split(both[:, width : width + rank_width])
    gp[:, 0:rank_width] = g_high
    gp[:, rank_width:two] = g_low
    gp[:, two : 3 * rank_width] = g_high

    @pl.loop(1, ng)
    def _(k):
        z_copy(k, lax.rem(my_g + k, ng)).wait()

    @pl.when(side == 1)
    def _():
        kout_copy.wait_recv()

    zcat = zall[...].reshape(units, width)
    part = dot(kout[...], jnp.concatenate([zcat, zcat], axis=0))
    psend[...] = part.astype(BF16).reshape(nb, two, width)

    def p_copy(k, b):
        return pltpu.make_async_remote_copy(
            src_ref=psend.at[b],
            dst_ref=precv.at[my_b],
            send_sem=p_send.at[k],
            recv_sem=p_recv.at[k],
            device_id=(side, my_g, b),
            device_id_type=MESH,
        )

    @pl.loop(1, nb)
    def _(k):
        p_copy(k, lax.rem(my_b + k, nb)).start()

    precv[my_b] = psend[my_b]
    side_copy.wait()
    for h in range(2):
        velocities_t[h * width : (h + 1) * width, :] = velocities[h].T

    @pl.loop(1, nb)
    def _(k):
        p_copy(k, lax.rem(my_b + k, nb)).wait()

    states = jnp.sum(precv[...].astype(F32), axis=0)
    s_high, s_low = split(states[0:rank_width])
    t_high, t_low = split(states[rank_width:two])
    rhs = jnp.concatenate([s_high, s_high, s_low, t_high, t_low], axis=0)
    potentials = (solved[...] - dot(gp[...], rhs)).astype(BF16)
    pot[...] = potentials
    weighted = (area[:, 0:1] * potentials.astype(F32)).astype(BF16)
    partial = dot(velocities_t[...], weighted).astype(BF16)
    held = msend.shape[1]
    if held != out_rows:
        row = lax.broadcasted_iota(jnp.int32, (nd * held, nd * out_rows), 0)
        col = lax.broadcasted_iota(jnp.int32, (nd * held, nd * out_rows), 1)
        home = (col // out_rows) * held + col % out_rows
        partial = dot(jnp.where(row == home, 1.0, 0.0).astype(BF16), partial).astype(BF16)
    msend[...] = partial.reshape(nd, held, width)

    def m_copy(k, d):
        return pltpu.make_async_remote_copy(
            src_ref=msend.at[d],
            dst_ref=mrecv.at[me],
            send_sem=m_send.at[k],
            recv_sem=m_recv.at[k],
            device_id=(side, d // nb, lax.rem(d, nb)),
            device_id_type=MESH,
        )

    @pl.loop(1, nd)
    def _(k):
        m_copy(k, lax.rem(me + k, nd)).start()

    mrecv[me] = msend[me]

    @pl.loop(0, nd - 1)
    def _(k):
        source = k + 1
        vel_copy(source // nb, lax.rem(source, nb), my_g, my_b).wait_send()

    @pl.loop(1, nd)
    def _(k):
        m_copy(k, lax.rem(me + k, nd)).wait()

    @pl.when(side == 0)
    def _():
        kout_copy.wait_send()

    mass_ref[...] = jnp.sum(mrecv[...].astype(F32), axis=0)[0:out_rows]


def hand_over(pot_in, mass_in, pot_out, mass_out, sems):
    copies = (
        pltpu.make_async_copy(pot_in, pot_out, sems.at[0]),
        pltpu.make_async_copy(mass_in, mass_out, sems.at[1]),
    )
    for copy in copies:
        copy.start()
    for copy in copies:
        copy.wait()


def body(
    node_modes,
    node_index,
    interp,
    normals,
    counts,
    inverse_diag,
    lower_left,
    lower_right,
    upper_left,
    upper_right,
    ranks,
    areas,
):
    ng, nb = lax.axis_size("grp"), lax.axis_size("blk")
    nd = ng * nb
    nodes, width = node_modes.shape[1:]
    cap_given = node_index.shape[1] // nd
    cap = -(-cap_given // TILE) * TILE
    if cap != cap_given:

        def widen(part):
            lead = part.shape[0]
            spare = ((0, 0), (0, 0), (0, cap - cap_given))
            return jnp.pad(part.reshape(lead, nd, cap_given), spare).reshape(lead, nd * cap)

        node_index, interp, normals = widen(node_index), widen(interp), widen(normals)
    slots = nd * cap
    panels = inverse_diag.shape[0]
    rank_width = lower_left.shape[1]
    factors = [part.T for part in (lower_left, lower_right, upper_left, upper_right)]
    two = 2 * rank_width
    units = ng * two
    out_rows = 2 * width // nd
    held = -(-out_rows // TILE) * TILE
    areas = areas.reshape(1, panels)
    shapes = (
        jax.ShapeDtypeStruct((panels, width), BF16),
        jax.ShapeDtypeStruct((out_rows, width), F32),
    )
    hbm = pl.BlockSpec(memory_space=pltpu.HBM)
    smem = pl.BlockSpec(memory_space=pltpu.SMEM)
    vmem = pl.BlockSpec(memory_space=pltpu.VMEM)
    dma = pltpu.SemaphoreType.DMA
    factor = pltpu.VMEM((rank_width, panels), BF16)
    scratch = [
        pltpu.VMEM((3, nodes, width), BF16),
        pltpu.VMEM((4, slots), jnp.int32),
        pltpu.VMEM((4, slots), F32),
        pltpu.VMEM((3, slots), F32),
        pltpu.VMEM((panels, panels), BF16),
        factor,
        factor,
        factor,
        factor,
        pltpu.VMEM((1, panels), F32),
        pltpu.VMEM((4 + 4 * (nodes // NODE_TILE), slots), F32),
        pltpu.VMEM((3 * width, nodes), BF16),
        pltpu.VMEM((nodes, nb * cap), BF16),
        pltpu.VMEM((nd, cap, width), BF16),
        pltpu.VMEM((nd, cap, width), BF16),
        pltpu.VMEM((panels, slots), BF16),
        pltpu.VMEM((nd, rank_width, 4 * rank_width), F32),
        pltpu.VMEM((nd, 3 * rank_width, 3 * rank_width), BF16),
        pltpu.VMEM((nd, two, 4 * rank_width), F32),
        pltpu.VMEM((nd, rank_width, 4 * rank_width), F32),
        pltpu.VMEM((nb * two, 2 * units), BF16),
        pltpu.VMEM((2 * two, panels), BF16),
        pltpu.VMEM((panels, 5 * rank_width), BF16),
        pltpu.VMEM((panels, width + rank_width), BF16),
        pltpu.VMEM((panels, width), F32),
        pltpu.VMEM((2, panels, width), BF16),
        pltpu.VMEM((2 * width, panels), BF16),
        pltpu.VMEM((ng, two, width), BF16),
        pltpu.VMEM((nb, two, width), BF16),
        pltpu.VMEM((nb, two, width), BF16),
        pltpu.VMEM((nd, held, width), BF16),
        pltpu.VMEM((nd, held, width), BF16),
        dma((12,)),
        dma((nb,)),
        dma((nb,)),
        dma((ng,)),
        dma((ng,)),
        dma((ng, nb)),
        dma((ng, nb)),
        dma(()),
        dma(()),
        dma(()),
        dma(()),
        pltpu.SemaphoreType.REGULAR,
        dma((ng,)),
        dma((ng,)),
        dma((nb,)),
        dma((nb,)),
        dma((nd,)),
        dma((nd,)),
    ]
    potentials, mass = pl.pallas_call(
        functools.partial(kernel, ng, nb, cap, out_rows),
        out_shape=(pltpu.VMEM((panels, width), BF16), pltpu.VMEM((out_rows, width), F32)),
        in_specs=[hbm, hbm, hbm, hbm, smem, hbm, hbm, hbm, hbm, hbm, smem, hbm],
        out_specs=(vmem, vmem),
        scratch_shapes=scratch,
        compiler_params=pltpu.CompilerParams(
            collective_id=0, has_side_effects=True, vmem_limit_bytes=56 * 1024 * 1024
        ),
    )(
        node_modes,
        node_index,
        interp,
        normals,
        counts.reshape(1, nd),
        inverse_diag,
        *factors,
        ranks,
        areas,
    )
    return pl.pallas_call(
        hand_over,
        out_shape=shapes,
        in_specs=[vmem, vmem],
        out_specs=(hbm, hbm),
        scratch_shapes=[dma((2,))],
        compiler_params=pltpu.CompilerParams(vmem_limit_bytes=4 * 1024 * 1024),
    )(potentials, mass)


def solution(mesh):
    split_rows = P(("grp", "blk"), None)
    split_cols = P(None, ("grp", "blk"))
    in_specs = (
        P(None, ("grp", "blk"), "side"),
        split_cols,
        split_cols,
        split_cols,
        split_cols,
        split_rows,
        split_rows,
        split_rows,
        split_rows,
        split_rows,
        P(("grp", "blk")),
        P(("grp", "blk")),
    )
    out_specs = (P(("grp", "blk"), "side"), P(("grp", "blk"), "side"))
    return jax.shard_map(body, mesh=mesh, in_specs=in_specs, out_specs=out_specs, check_vma=False)
```

```python
import functools

import jax
import jax.numpy as jnp
from jax import lax
from jax.experimental import pallas as pl
from jax.experimental.pallas import tpu as pltpu
from jax.sharding import PartitionSpec as P

MESH = pl.DeviceIdType.MESH
F32 = jnp.float32
BF16 = jnp.bfloat16
TILE = 16
LANES = 128
NODE_TILE = 256


def dot(a, b):
    return jnp.dot(a, b, preferred_element_type=F32)


def dot_rows(a, b):
    return lax.dot_general(a, b, (((0,), (0,)), ((), ())), preferred_element_type=F32)


def dot_lanes(a, b):
    return lax.dot_general(a, b, (((1,), (1,)), ((), ())), preferred_element_type=F32)


def split(a):
    high = a.astype(BF16)
    return high, (a - high.astype(F32)).astype(BF16)


def kernel(
    ng,
    nb,
    cap,
    out_rows,
    modes_hbm,
    index_hbm,
    interp_hbm,
    normals_hbm,
    counts,
    diag_hbm,
    ll_hbm,
    lr_hbm,
    ul_hbm,
    ur_hbm,
    ranks,
    areas_hbm,
    pot,
    mass_ref,
    modes,
    index,
    interp,
    normals,
    diag,
    ll,
    lr,
    ul,
    ur,
    areas,
    rows_pack,
    modes_t,
    wbuf,
    sendbuf,
    arrived,
    pick,
    maps,
    left,
    record,
    back_terms,
    kout,
    wcat,
    gp,
    bu,
    solved,
    velocities,
    velocities_t,
    zall,
    psend,
    precv,
    msend,
    mrecv,
    local_sem,
    map_send,
    map_recv,
    slab_send,
    slab_recv,
    vel_send,
    vel_recv,
    side_send,
    side_recv,
    k_send,
    k_recv,
    ready,
    z_send,
    z_recv,
    p_send,
    p_recv,
    m_send,
    m_recv,
):
    nd = ng * nb
    rank_width = ll.shape[0]
    two = 2 * rank_width
    panels = diag.shape[0]
    nodes, width = modes.shape[1:]
    slots = nd * cap
    side, my_g, my_b = lax.axis_index("side"), lax.axis_index("grp"), lax.axis_index("blk")
    me = my_g * nb + my_b

    barrier = pltpu.get_barrier_semaphore()

    @pl.loop(1, nd)
    def _(k):
        other = lax.rem(me + k, nd)
        pl.semaphore_signal(
            barrier, inc=1, device_id=(side, other // nb, lax.rem(other, nb)), device_id_type=MESH
        )

    other_side = (1 - side, my_g, my_b)

    @pl.when(side == 0)
    def _():
        pl.semaphore_signal(barrier, inc=1, device_id=other_side, device_id_type=MESH)

    pairs = [
        (diag_hbm, diag),
        (lr_hbm, lr),
        (ur_hbm, ur),
        (ll_hbm, ll),
        (ul_hbm, ul),
        (index_hbm, index),
        (interp_hbm, interp),
        (normals_hbm, normals),
        (areas_hbm, areas),
    ] + [(modes_hbm.at[c], modes.at[c]) for c in range(3)]
    loads = [pltpu.make_async_copy(a, b, local_sem.at[i]) for i, (a, b) in enumerate(pairs)]
    for load in (*loads[5:8], *loads[9:12], *loads[0:5], loads[8]):
        load.start()

    for i in (5, 6, 7):
        loads[i].wait()
    tile_of = index[...] // NODE_TILE
    rows_pack[0:4, :] = (index[...] - tile_of * NODE_TILE).astype(F32)
    for tile in range(nodes // NODE_TILE):
        rows_pack[4 * tile + 4 : 4 * tile + 8, :] = jnp.where(tile_of == tile, interp[...], 0.0)

    def map_copy(k, b):
        return pltpu.make_async_remote_copy(
            src_ref=maps.at[me],
            dst_ref=maps.at[me],
            send_sem=map_send.at[k],
            recv_sem=map_recv.at[k],
            device_id=(side, my_g, b),
            device_id_type=MESH,
        )

    def slab_copy(k, g):
        return pltpu.make_async_remote_copy(
            src_ref=maps.at[pl.ds(my_g * nb, nb)],
            dst_ref=maps.at[pl.ds(my_g * nb, nb)],
            send_sem=slab_send.at[k],
            recv_sem=slab_recv.at[k],
            device_id=(side, g, my_b),
            device_id_type=MESH,
        )

    def vel_copy(kg, kb, g, b):
        return pltpu.make_async_remote_copy(
            src_ref=sendbuf.at[g * nb + b],
            dst_ref=arrived.at[me],
            send_sem=vel_send.at[kg, kb],
            recv_sem=vel_recv.at[kg, kb],
            device_id=(side, g, b),
            device_id_type=MESH,
        )

    chunk = nb * cap
    node_ids = [
        (lax.broadcasted_iota(jnp.int32, (TILE, LANES), 0) + part * TILE).astype(F32).astype(BF16)
        for part in range(NODE_TILE // TILE)
    ]
    zero16 = jnp.zeros((TILE, LANES), BF16)

    def weights(g):
        @pl.loop(0, chunk // LANES)
        def _(q):
            here = pl.ds(pl.multiple_of(g * chunk + q * LANES, LANES), LANES)
            there = pl.ds(pl.multiple_of(q * LANES, LANES), LANES)

            def wide(r):
                row = rows_pack[r : r + 1, here]
                return jnp.broadcast_to(row, (TILE, LANES)).astype(BF16)

            places = [wide(k) for k in range(4)]
            for tile in range(nodes // NODE_TILE):
                worth = [wide(4 * tile + 4 + k) for k in range(4)]
                for part, ids in enumerate(node_ids):
                    terms = [jnp.where(ids == places[k], worth[k], zero16) for k in range(4)]
                    start = tile * NODE_TILE + part * TILE
                    wbuf[start : start + TILE, there] = (terms[0] + terms[1]) + (terms[2] + terms[3])

    def velocity_chunk(g):
        weights(g)
        moved = dot(modes_t[...], wbuf[...])
        normal = normals[:, pl.ds(pl.multiple_of(g * chunk, LANES), chunk)]
        velocity = normal[0:1] * moved[0:width]
        for c in (1, 2):
            velocity += normal[c : c + 1] * moved[c * width : (c + 1) * width]
        sendbuf[pl.ds(g * nb, nb)] = velocity.T.astype(BF16).reshape(nb, cap, width)

    def velocity_send(kg, g):
        @pl.loop(1, jnp.where(kg == 0, nb, nb + 1))
        def _(k):
            vel_copy(kg, lax.rem(k, nb), g, lax.rem(my_b + k, nb)).start()

    first = lax.rem(my_g + 1, ng)
    for i in (9, 10, 11):
        loads[i].wait()
    for c in range(3):
        modes_t[c * width : (c + 1) * width, :] = modes[c].T
    velocity_chunk(first)
    pl.semaphore_wait(barrier, nd - 1 + side)

    @pl.when(side == 1)
    def _():
        pl.semaphore_signal(ready, inc=1, device_id=other_side, device_id_type=MESH)

    velocity_send(lax.rem(jnp.int32(1), ng), first)

    def prepare():
        for i in range(5):
            loads[i].wait()
        keep = lax.broadcasted_iota(jnp.int32, (rank_width, panels), 0) < ranks[0]
        lower = jnp.where(keep, ll[...].astype(F32), 0.0).astype(BF16)
        upper = jnp.where(keep, ul[...].astype(F32), 0.0).astype(BF16)
        right = jnp.concatenate([lr[...], ur[...]], axis=0)
        w_high, w_low = split(dot(right, diag[...]))
        wcat[0:two, :] = w_high
        wcat[two : 2 * two, :] = w_low
        @pl.when(side == 0)
        def _():
            both = dot_lanes(wcat[...], lower)
            both = both[0:two] + both[two : 2 * two]
            top = dot_lanes(ur[...], upper)
            maps[me] = jnp.concatenate(
                [both[0:rank_width], both[rank_width:two], top, jnp.zeros_like(top)], axis=1
            )

            @pl.loop(1, nb)
            def _(k):
                map_copy(k, lax.rem(my_b + k, nb)).start()

        lower_t = lower.astype(F32).T.astype(BF16)
        upper_t = upper.astype(F32).T.astype(BF16)
        bu[:, width : width + rank_width] = lower_t
        gp[:, 3 * rank_width : 4 * rank_width] = upper_t
        gp[:, 4 * rank_width : 5 * rank_width] = upper_t

    pl.when(side == 0)(prepare)

    def rest(step):
        kg = lax.rem(step + 1, ng)
        g = lax.rem(my_g + kg, ng)
        velocity_chunk(g)
        velocity_send(kg, g)

    rest(jnp.int32(1))

    @pl.when(side == 0)
    def _():
        @pl.loop(1, nb)
        def _(k):
            map_copy(k, lax.rem(my_b + k, nb)).wait()

        @pl.loop(1, ng)
        def _(k):
            slab_copy(k, lax.rem(my_g + k, ng)).start()

    pl.loop(2, ng)(rest)

    pl.when(side == 1)(prepare)
    arrived[me] = sendbuf[me]

    slot_ids = lax.broadcasted_iota(jnp.int32, (1, slots), 1)

    def place(j, carry):
        offset, target = carry
        local = slot_ids - j * cap
        count = counts[0, j]
        target = jnp.where((local >= 0) & (local < count), local + offset, target)
        return offset + count, target

    _, target = lax.fori_loop(
        0, nd, place, (jnp.int32(0), jnp.full((1, slots), -1, jnp.int32))
    )
    panel_ids = lax.broadcasted_iota(jnp.int32, (TILE, slots), 0)

    per_step = panels // TILE // (2 * nb)

    def pick_rows(step):
        for r in range(per_step):
            i = step * per_step + r
            hot = jnp.where(panel_ids + i * TILE == target, 1.0, 0.0)
            pick[pl.ds(pl.multiple_of(i * TILE, TILE), TILE), :] = hot.astype(BF16)

    @pl.when(side == 1)
    def _():
        pl.loop(0, 2 * nb)(pick_rows)

    kout_copy = pltpu.make_async_remote_copy(
        src_ref=kout,
        dst_ref=kout,
        send_sem=k_send,
        recv_sem=k_recv,
        device_id=other_side,
        device_id_type=MESH,
    )
    units = ng * two
    span = 4 * rank_width

    @pl.when(side == 0)
    def _():
        @pl.loop(1, ng)
        def _(k):
            slab_copy(k, lax.rem(my_g + k, ng)).wait()

        def three(high, low):
            return jnp.concatenate([high, low, high], axis=1)

        def state(s):
            high, low = split(s)
            return jnp.concatenate([high, high, low], axis=0)

        @pl.loop(0, nd, unroll=4)
        def _(i):
            high, low = split(maps[i])
            for c in range(3):
                part = slice(c * rank_width, (c + 1) * rank_width)
                left[i, part, :] = three(high[:, part], low[:, part])

        row_id = lax.broadcasted_iota(jnp.int32, (rank_width, span), 0)
        col_id = lax.broadcasted_iota(jnp.int32, (rank_width, span), 1)

        def unit(place):
            return jnp.where(col_id == row_id + place * rank_width, 1.0, 0.0)

        def forward(b, states):
            hit = jnp.where(b == my_b, 1.0, 0.0)
            after = []
            for g in range(ng):
                i = g * nb + b
                record[i, 0:rank_width, :] = states[g]
                moved = dot(left[i, 0:two, :], state(states[g]))
                back_terms[i] = moved[rank_width:two]
                after.append(states[g] - moved[0:rank_width] + hit * unit(2))
            pick_rows(b)
            return tuple(after)

        def backward(step, states):
            b = nb - 1 - step
            hit = jnp.where(b == my_b, 1.0, 0.0)
            after = []
            for g in range(ng):
                i = g * nb + b
                record[i, rank_width:two, :] = states[g]
                moved = dot(left[i, two : 3 * rank_width, :], state(states[g]))
                after.append(states[g] + (hit * unit(3) - back_terms[i]) - moved)
            pick_rows(nb + step)
            return tuple(after)

        ahead = lax.fori_loop(0, nb, forward, (unit(1),) * ng)
        behind = lax.fori_loop(0, nb, backward, (unit(0),) * ng)

        row_two = lax.broadcasted_iota(jnp.int32, (two, units), 0)
        col_two = lax.broadcasted_iota(jnp.int32, (two, units), 1)

        def terms_of(g):
            return jnp.where(col_two == row_two + two * g, 1.0, 0.0).astype(BF16)

        nothing = jnp.zeros((rank_width, units), F32)

        def across(lhs, t, s, g):
            l_high, l_low = split(lhs)
            t_high, t_low = split(t)
            s_high, s_low = split(s)
            own = terms_of(g)
            high = jnp.concatenate([t_high, s_high, own], axis=0)
            low = jnp.concatenate([t_low, s_low, jnp.zeros_like(own)], axis=0)
            return dot(l_high, high) + dot(l_low, high) + dot(l_high, low)

        s_in, t_in = [nothing], [nothing]
        for g in range(ng - 1):
            s_in.append(across(ahead[g], nothing, s_in[g], g))
        for g in range(ng - 1, 0, -1):
            t_in.append(across(behind[g], t_in[-1], s_in[g], g))
        t_in = t_in[::-1]
        s_here, t_here = nothing, nothing
        for g in range(ng):
            s_here = jnp.where(my_g == g, s_in[g], s_here)
            t_here = jnp.where(my_g == g, t_in[g], t_here)
        mine = record[pl.ds(my_g * nb, nb)].reshape(nb * two, span)
        k_high, k_low = split(across(mine, t_here, s_here, my_g))
        kout[:, 0:units] = k_high
        kout[:, units : 2 * units] = k_low
        pl.semaphore_wait(ready, 1)
        kout_copy.start()

    loads[8].wait()
    area = areas[...].T

    @pl.loop(0, nd - 1)
    def _(k):
        source = k + 1
        vel_copy(source // nb, lax.rem(source, nb), my_g, my_b).wait_recv()

    b = dot(pick[...], arrived[...].reshape(slots, width)).astype(BF16)
    velocities[side] = b
    side_copy = pltpu.make_async_remote_copy(
        src_ref=velocities.at[side],
        dst_ref=velocities.at[side],
        send_sem=side_send,
        recv_sem=side_recv,
        device_id=(1 - side, my_g, my_b),
        device_id_type=MESH,
    )
    z = dot(wcat[...], b)
    zall[my_g] = (z[0:two] + z[two : 2 * two]).astype(BF16)

    def z_copy(k, g):
        return pltpu.make_async_remote_copy(
            src_ref=zall.at[my_g],
            dst_ref=zall.at[my_g],
            send_sem=z_send.at[k],
            recv_sem=z_recv.at[k],
            device_id=(side, g, my_b),
            device_id_type=MESH,
        )

    @pl.loop(1, ng)
    def _(k):
        z_copy(k, lax.rem(my_g + k, ng)).start()

    side_copy.start()
    bu[:, 0:width] = b
    both = dot(diag[...], bu[...])
    solved[...] = both[:, 0:width]
    g_high, g_low = split(both[:, width : width + rank_width])
    gp[:, 0:rank_width] = g_high
    gp[:, rank_width:two] = g_low
    gp[:, two : 3 * rank_width] = g_high

    @pl.loop(1, ng)
    def _(k):
        z_copy(k, lax.rem(my_g + k, ng)).wait()

    @pl.when(side == 1)
    def _():
        kout_copy.wait_recv()

    zcat = zall[...].reshape(units, width)
    part = dot(kout[...], jnp.concatenate([zcat, zcat], axis=0))
    psend[...] = part.astype(BF16).reshape(nb, two, width)

    def p_copy(k, b):
        return pltpu.make_async_remote_copy(
            src_ref=psend.at[b],
            dst_ref=precv.at[my_b],
            send_sem=p_send.at[k],
            recv_sem=p_recv.at[k],
            device_id=(side, my_g, b),
            device_id_type=MESH,
        )

    @pl.loop(1, nb)
    def _(k):
        p_copy(k, lax.rem(my_b + k, nb)).start()

    precv[my_b] = psend[my_b]
    side_copy.wait()
    for h in range(2):
        velocities_t[h * width : (h + 1) * width, :] = velocities[h].T

    @pl.loop(1, nb)
    def _(k):
        p_copy(k, lax.rem(my_b + k, nb)).wait()

    states = jnp.sum(precv[...].astype(F32), axis=0)
    s_high, s_low = split(states[0:rank_width])
    t_high, t_low = split(states[rank_width:two])
    rhs = jnp.concatenate([s_high, s_high, s_low, t_high, t_low], axis=0)
    potentials = (solved[...] - dot(gp[...], rhs)).astype(BF16)
    pot[...] = potentials
    weighted = (area[:, 0:1] * potentials.astype(F32)).astype(BF16)
    partial = dot(velocities_t[...], weighted).astype(BF16)
    held = msend.shape[1]
    if held != out_rows:
        row = lax.broadcasted_iota(jnp.int32, (nd * held, nd * out_rows), 0)
        col = lax.broadcasted_iota(jnp.int32, (nd * held, nd * out_rows), 1)
        home = (col // out_rows) * held + col % out_rows
        partial = dot(jnp.where(row == home, 1.0, 0.0).astype(BF16), partial).astype(BF16)
    msend[...] = partial.reshape(nd, held, width)

    def m_copy(k, d):
        return pltpu.make_async_remote_copy(
            src_ref=msend.at[d],
            dst_ref=mrecv.at[me],
            send_sem=m_send.at[k],
            recv_sem=m_recv.at[k],
            device_id=(side, d // nb, lax.rem(d, nb)),
            device_id_type=MESH,
        )

    @pl.loop(1, nd)
    def _(k):
        m_copy(k, lax.rem(me + k, nd)).start()

    mrecv[me] = msend[me]

    @pl.loop(0, nd - 1)
    def _(k):
        source = k + 1
        vel_copy(source // nb, lax.rem(source, nb), my_g, my_b).wait_send()

    @pl.loop(1, nd)
    def _(k):
        m_copy(k, lax.rem(me + k, nd)).wait()

    @pl.when(side == 0)
    def _():
        kout_copy.wait_send()

    mass_ref[...] = jnp.sum(mrecv[...].astype(F32), axis=0)[0:out_rows]


def hand_over(pot_in, mass_in, pot_out, mass_out, sems):
    copies = (
        pltpu.make_async_copy(pot_in, pot_out, sems.at[0]),
        pltpu.make_async_copy(mass_in, mass_out, sems.at[1]),
    )
    for copy in copies:
        copy.start()
    for copy in copies:
        copy.wait()


def body(
    node_modes,
    node_index,
    interp,
    normals,
    counts,
    inverse_diag,
    lower_left,
    lower_right,
    upper_left,
    upper_right,
    ranks,
    areas,
):
    ng, nb = lax.axis_size("grp"), lax.axis_size("blk")
    nd = ng * nb
    nodes, width = node_modes.shape[1:]
    cap_given = node_index.shape[1] // nd
    cap = -(-cap_given // TILE) * TILE
    if cap != cap_given:

        def widen(part):
            lead = part.shape[0]
            spare = ((0, 0), (0, 0), (0, cap - cap_given))
            return jnp.pad(part.reshape(lead, nd, cap_given), spare).reshape(lead, nd * cap)

        node_index, interp, normals = widen(node_index), widen(interp), widen(normals)
    slots = nd * cap
    panels = inverse_diag.shape[0]
    rank_width = lower_left.shape[1]
    factors = [part.T for part in (lower_left, lower_right, upper_left, upper_right)]
    two = 2 * rank_width
    units = ng * two
    out_rows = 2 * width // nd
    held = -(-out_rows // TILE) * TILE
    areas = areas.reshape(1, panels)
    shapes = (
        jax.ShapeDtypeStruct((panels, width), BF16),
        jax.ShapeDtypeStruct((out_rows, width), F32),
    )
    hbm = pl.BlockSpec(memory_space=pltpu.HBM)
    smem = pl.BlockSpec(memory_space=pltpu.SMEM)
    vmem = pl.BlockSpec(memory_space=pltpu.VMEM)
    dma = pltpu.SemaphoreType.DMA
    factor = pltpu.VMEM((rank_width, panels), BF16)
    scratch = [
        pltpu.VMEM((3, nodes, width), BF16),
        pltpu.VMEM((4, slots), jnp.int32),
        pltpu.VMEM((4, slots), F32),
        pltpu.VMEM((3, slots), F32),
        pltpu.VMEM((panels, panels), BF16),
        factor,
        factor,
        factor,
        factor,
        pltpu.VMEM((1, panels), F32),
        pltpu.VMEM((4 + 4 * (nodes // NODE_TILE), slots), F32),
        pltpu.VMEM((3 * width, nodes), BF16),
        pltpu.VMEM((nodes, nb * cap), BF16),
        pltpu.VMEM((nd, cap, width), BF16),
        pltpu.VMEM((nd, cap, width), BF16),
        pltpu.VMEM((panels, slots), BF16),
        pltpu.VMEM((nd, rank_width, 4 * rank_width), F32),
        pltpu.VMEM((nd, 3 * rank_width, 3 * rank_width), BF16),
        pltpu.VMEM((nd, two, 4 * rank_width), F32),
        pltpu.VMEM((nd, rank_width, 4 * rank_width), F32),
        pltpu.VMEM((nb * two, 2 * units), BF16),
        pltpu.VMEM((2 * two, panels), BF16),
        pltpu.VMEM((panels, 5 * rank_width), BF16),
        pltpu.VMEM((panels, width + rank_width), BF16),
        pltpu.VMEM((panels, width), F32),
        pltpu.VMEM((2, panels, width), BF16),
        pltpu.VMEM((2 * width, panels), BF16),
        pltpu.VMEM((ng, two, width), BF16),
        pltpu.VMEM((nb, two, width), BF16),
        pltpu.VMEM((nb, two, width), BF16),
        pltpu.VMEM((nd, held, width), BF16),
        pltpu.VMEM((nd, held, width), BF16),
        dma((12,)),
        dma((nb,)),
        dma((nb,)),
        dma((ng,)),
        dma((ng,)),
        dma((ng, nb)),
        dma((ng, nb)),
        dma(()),
        dma(()),
        dma(()),
        dma(()),
        pltpu.SemaphoreType.REGULAR,
        dma((ng,)),
        dma((ng,)),
        dma((nb,)),
        dma((nb,)),
        dma((nd,)),
        dma((nd,)),
    ]
    potentials, mass = pl.pallas_call(
        functools.partial(kernel, ng, nb, cap, out_rows),
        out_shape=(pltpu.VMEM((panels, width), BF16), pltpu.VMEM((out_rows, width), F32)),
        in_specs=[hbm, hbm, hbm, hbm, smem, hbm, hbm, hbm, hbm, hbm, smem, hbm],
        out_specs=(vmem, vmem),
        scratch_shapes=scratch,
        compiler_params=pltpu.CompilerParams(
            collective_id=0, has_side_effects=True, vmem_limit_bytes=56 * 1024 * 1024
        ),
    )(
        node_modes,
        node_index,
        interp,
        normals,
        counts.reshape(1, nd),
        inverse_diag,
        *factors,
        ranks,
        areas,
    )
    return pl.pallas_call(
        hand_over,
        out_shape=shapes,
        in_specs=[vmem, vmem],
        out_specs=(hbm, hbm),
        scratch_shapes=[dma((2,))],
        compiler_params=pltpu.CompilerParams(vmem_limit_bytes=4 * 1024 * 1024),
    )(potentials, mass)


def solution(mesh):
    split_rows = P(("grp", "blk"), None)
    split_cols = P(None, ("grp", "blk"))
    in_specs = (
        P(None, ("grp", "blk"), "side"),
        split_cols,
        split_cols,
        split_cols,
        split_cols,
        split_rows,
        split_rows,
        split_rows,
        split_rows,
        split_rows,
        P(("grp", "blk")),
        P(("grp", "blk")),
    )
    out_specs = (P(("grp", "blk"), "side"), P(("grp", "blk"), "side"))
    return jax.shard_map(body, mesh=mesh, in_specs=in_specs, out_specs=out_specs, check_vma=False)
```
